128 devices in a mesh: dp: 16 (over y_lo, x, core), feat: 8 (over y_hi, z).
Axes of the slice: x: 4, y: 4 (y_hi: 2, y_lo: 2; y = y_hi * 2 + y_lo), z: 4, core: 2. Of those that a mesh axis runs over, the one named last changes fastest.
Arguments:
- states: bfloat16 [256, 32, 32768], P('dp', None, 'feat'), may hold values from -2000 to 2000
- token_ids: int32 [256, 32], P('dp'), may hold values from 0 to 16383
- crop_start: int32 [2, 256], P(None, 'dp'), may hold values from 0 to 24, as said below
- crop_len: int32 [2, 256], P(None, 'dp'), may hold values from 8 to 32, as said below
- item_weight: float32 [16384], replicated, may hold values from 0.25 to 4
Outputs:
- grad_first: float32 [256, 32768], P('dp', 'feat')
- grad_second: float32 [256, 32768], P('dp', 'feat')
- loss_rows: float32 [32768], P('feat')
The draws below stay inside these ranges and needn't reach their ends.
Inputs may be any that keep to these rules, and one draw needn't show every extreme that they name: crop_start + crop_len <= 32 for every view and session. `crop_len`: in each view some session's crop spans all 32 positions.
All inputs are finite; a program needn't handle non-finite values.
Results may differ from the reference program's by a relative error of at most 0.015.
Values may be sent and summed in bfloat16 or wider, within the bound.
No kernel may reach another device: no remote copies, remote signals or barrier semaphores. Data moves between devices by JAX's collectives and lax.ppermute only.
A program may use at most 128 MiB of HBM per device.

```python
import math
import jax
import jax.numpy as jnp
import numpy as np
from jax import lax

F = 32768
L = 32
VOCAB = 16384
SESSIONS = 256


def crop_pair(key):
    key_len, key_pick, key_start = jax.random.split(key, 3)
    length = jax.random.randint(key_len, (2, SESSIONS), L // 4, L + 1)
    chosen = jax.random.randint(key_pick, (2, 1), 0, SESSIONS)
    shortest = (chosen + 1) % SESSIONS
    slots = lax.broadcasted_iota(jnp.int32, (2, SESSIONS), 1)
    length = jnp.where(slots == chosen, L, length)
    length = jnp.where(slots == shortest, L // 4, length)
    start = jax.random.randint(key_start, (2, SESSIONS), 0, L) % (L - length + 1)
    start = jnp.where(slots == shortest, L - L // 4, start)
    return (start.astype(jnp.int32), length.astype(jnp.int32))


def draw_crop_start(key, part):
    start, length = crop_pair(key)
    return start


def draw_crop_len(key, part):
    start, length = crop_pair(key)
    return length


def draw_states(key, part):
    key = jax.random.fold_in(key, 11)
    key_sess, key_feat, key_base = jax.random.split(key, 3)
    position = jnp.arange(SESSIONS, dtype=jnp.float32) / (SESSIONS - 1)
    session_scale = (1.0 + 2.0 * position) * jnp.exp(jax.random.uniform(key_sess, (SESSIONS,), minval=0.0, maxval=math.log(10.0)))
    feature_scale = jnp.exp(jax.random.uniform(key_feat, (F,), minval=0.0, maxval=math.log(10.0)))
    base_part = jnp.clip(jax.random.normal(key_base, (SESSIONS, L, F)), -6.0, 6.0)
    values = base_part * session_scale[:, None, None] * feature_scale
    return values.astype(jnp.bfloat16)


def touch_ends(array, rng, smallest, top_value):
    dims = array.shape
    spot = [jax.random.randint(jax.random.fold_in(rng, axis), (), 0, dims[axis]) for axis in range(len(dims))]
    array = array.at[tuple(spot)].set(smallest)
    longest = dims.index(max(dims))
    spot[longest] = (spot[longest] + 1) % dims[longest]
    return array.at[tuple(spot)].set(top_value)


def rank_bounds(number_of, skew):
    weights = [(1 << 20) // math.isqrt(rank ** skew) + 1 for rank in range(1, number_of + 1)]
    deviation = 1 + sum(weights) // (1 << 30)
    return np.cumsum(np.array([max(1, weight // deviation) for weight in weights]))


def ranked(rng, shape, count, lean):
    grid = rank_bounds(count, lean)
    lot = jax.random.randint(jax.random.fold_in(rng, 1), shape, 0, int(grid[count - 1]))
    standing = jnp.searchsorted(jnp.asarray(grid, jnp.int32), lot, side="right")
    return jax.random.permutation(jax.random.fold_in(rng, 2), count)[standing].astype(jnp.int32)


def setup_inputs(seed: int = 0) -> dict:
    keys = jax.random.split(jax.random.key(seed), 6)
    return {
        "states": draw_states(jax.random.fold_in(keys[5], 71), 0),
        "token_ids": touch_ends(ranked(keys[1], (SESSIONS, L), VOCAB, 2), jax.random.fold_in(keys[1], 3), 0, VOCAB - 1).astype(jnp.int32),
        "crop_start": draw_crop_start(jax.random.fold_in(keys[5], 71), 0),
        "crop_len": draw_crop_len(jax.random.fold_in(keys[5], 71), 0),
        "item_weight": jnp.clip(jnp.exp(jax.random.uniform(keys[4], (VOCAB,), jnp.float32, math.log(0.25), math.log(4.0))), 0.25, 4.0),
    }


off_weight = 0.0051
eps_norm = 1e-05

def pool_views(states, token_ids, crop_start, crop_len, item_weight):
    token_weight = item_weight[token_ids]
    places = lax.broadcasted_iota(jnp.int32, (2, token_ids.shape[0], token_ids.shape[1]), 2)
    inside = (places >= crop_start[:, :, None]) & (places < (crop_start + crop_len)[:, :, None])
    masked = jnp.where(inside, token_weight[None], jnp.float32(0.0))
    coefficients = (masked / lax.optimization_barrier(jnp.sum(masked, axis=2, keepdims=True))).astype(jnp.bfloat16)
    view_pair = jnp.einsum('vbl,blf->vbf', coefficients.astype(jnp.float32), states.astype(jnp.float32), precision=lax.Precision.HIGHEST)
    return view_pair.astype(jnp.bfloat16)

def normalize(rows):
    values = rows.astype(jnp.float32)
    row_count = rows.shape[0]
    col_mean = lax.optimization_barrier(jnp.sum(values, axis=0)) / row_count
    col_var = lax.optimization_barrier(jnp.sum(values * values, axis=0)) / row_count - col_mean * col_mean
    inv_scale = lax.rsqrt(col_var + eps_norm)
    centered = (values - col_mean) * inv_scale
    return (centered, centered.astype(jnp.bfloat16), inv_scale)

def finish(grad_part, centered, inv_scale, row_count):
    sum_part = lax.optimization_barrier(jnp.sum(grad_part, axis=0))
    dot_part = lax.optimization_barrier(jnp.sum(grad_part * centered, axis=0))
    return inv_scale * (grad_part - sum_part / row_count - centered * (dot_part / row_count))

def reference(states, token_ids, crop_start, crop_len, item_weight):
    view_pair = pool_views(states, token_ids, crop_start, crop_len, item_weight)
    centered_one, normed_one, scale_one = normalize(view_pair[0])
    centered_two, normed_two, scale_two = normalize(view_pair[1])
    row_count = view_pair.shape[1]
    gram_one = jnp.dot(normed_one, normed_one.T, preferred_element_type=jnp.float32)
    gram_two = jnp.dot(normed_two, normed_two.T, preferred_element_type=jnp.float32)
    wide_one = normed_one.astype(jnp.float32)
    wide_two = normed_two.astype(jnp.float32)
    diagonal = lax.optimization_barrier(jnp.sum(wide_one * wide_two, axis=0)) / row_count
    mixed_one = jnp.dot(gram_two, wide_one, precision=lax.Precision.HIGHEST)
    mixed_two = jnp.dot(gram_one, wide_two, precision=lax.Precision.HIGHEST)
    row_square = lax.optimization_barrier(jnp.sum(wide_one * mixed_one, axis=0)) / (row_count * row_count)
    loss_rows = (1.0 - diagonal) * (1.0 - diagonal) + off_weight * (row_square - diagonal * diagonal)
    diag_shift = 2.0 * (diagonal - 1.0) - 2.0 * off_weight * diagonal
    grad_part_one = 2.0 * off_weight / row_count * mixed_one + diag_shift * wide_two
    grad_part_two = 2.0 * off_weight / row_count * mixed_two + diag_shift * wide_one
    grad_first = finish(grad_part_one, centered_one, scale_one, row_count)
    grad_second = finish(grad_part_two, centered_two, scale_two, row_count)
    return (grad_first, grad_second, loss_rows)
```

```python
import functools

import jax
import jax.numpy as jnp
from jax import lax
from jax.experimental import pallas as pl
from jax.experimental.pallas import tpu as pltpu
from jax.sharding import Mesh
from jax.sharding import PartitionSpec as P

off_weight = 0.0051
eps_norm = 1e-05

f32 = jnp.float32
bf16 = jnp.bfloat16

DP = ("yl", "x", "c")
FEAT = ("yh", "z")
WIDE = 512
LANES = 128


def iota(shape, dim):
    return lax.broadcasted_iota(jnp.int32, shape, dim)


def params():
    return pltpu.CompilerParams(vmem_limit_bytes=24 * 1024 * 1024)


def total(values):
    return jnp.sum(values, axis=0, keepdims=True)


def scaled(values):
    count = values.shape[0]
    mean = total(values) / count
    var = total(values * values) / count - mean * mean
    return mean, lax.rsqrt(var + eps_norm)


def coefficient_rows(ids, start, length, table):
    sessions, tokens = ids.shape
    cols = sessions * tokens
    spread = jnp.where(iota((tokens, cols), 1) % tokens == iota((tokens, cols), 0), 1.0, 0.0).astype(bf16)
    own = iota((sessions, cols), 1) // tokens == iota((sessions, cols), 0)

    def in_line(small):
        rows = jnp.dot(small.astype(f32).astype(bf16), spread, preferred_element_type=f32)
        return total(jnp.where(own, rows, 0.0))

    high, low = in_line(ids // LANES), in_line(ids % LANES)
    place = iota((LANES, cols), 0).astype(f32)
    pick_high = jnp.where(place == high, 1.0, 0.0).astype(bf16)
    first = table.astype(bf16)
    rest = table - first.astype(f32)
    second = rest.astype(bf16)
    third = (rest - second.astype(f32)).astype(bf16)
    found = jnp.zeros((LANES, cols), f32)
    for part in (first, second, third):
        found = found + lax.dot_general(part, pick_high, (((0,), (0,)), ((), ())), preferred_element_type=f32)
    weight = total(jnp.where(place == low, found, 0.0))

    def column(pair):
        spread_rows = jnp.concatenate(
            [jnp.broadcast_to(pair[v : v + 1].astype(f32), (sessions, sessions)) for v in range(2)], axis=0
        )
        square = (2 * sessions, sessions)
        mine = iota(square, 0) % sessions == iota(square, 1)
        return jnp.sum(jnp.where(mine, spread_rows, 0.0), axis=1, keepdims=True)

    first_place, past = column(start), column(start + length)
    shape = (2 * sessions, cols)
    col = iota(shape, 1)
    token = (col % tokens).astype(f32)
    inside = (col // tokens == iota(shape, 0) % sessions) & (token >= first_place) & (token < past)
    masked = jnp.where(inside, weight, 0.0)
    return (masked / jnp.sum(masked, axis=1, keepdims=True)).astype(bf16)


def pool_kernel(ids_ref, start_ref, len_ref, table_ref, states_ref, out_ref, coef_ref):
    @pl.when(pl.program_id(0) == 0)
    def _():
        coef_ref[...] = coefficient_rows(ids_ref[...], start_ref[...], len_ref[...], table_ref[...])

    sessions, tokens, width = states_ref.shape
    block = states_ref[...].reshape(sessions * tokens, width)
    views = jnp.dot(coef_ref[...], block, preferred_element_type=f32).astype(bf16)
    for x in range(out_ref.shape[1]):
        out_ref[0, x, 0] = views[sessions:]
        out_ref[0, x, 1] = views[:sessions]


def pool(states, token_ids, crop_start, crop_len, item_weight, x_size):
    sessions, tokens, feats = states.shape
    table = item_weight.reshape(-1, LANES)
    half = feats // 2
    per_half = half // WIDE
    whole = lambda array: pl.BlockSpec(array.shape, lambda k: (0,) * array.ndim)
    return pl.pallas_call(
        pool_kernel,
        grid=(feats // WIDE,),
        in_specs=[
            whole(token_ids),
            whole(crop_start),
            whole(crop_len),
            whole(table),
            pl.BlockSpec((sessions, tokens, WIDE), lambda k: (0, 0, k)),
        ],
        out_specs=pl.BlockSpec((1, x_size, 2, sessions, WIDE), lambda k: (k // per_half, 0, 0, 0, k % per_half)),
        out_shape=jax.ShapeDtypeStruct((2, x_size, 2, sessions, half), bf16),
        scratch_shapes=[pltpu.VMEM((2 * sessions, sessions * tokens), bf16)],
        compiler_params=params(),
        name="pool",
    )(token_ids, crop_start, crop_len, table, states)


def triangle():
    shape = (LANES, LANES)
    return iota(shape, 0), iota(shape, 1)


def store_packed(out_ref, corner, mixed, diag):
    out_ref[0:LANES, :] = corner.astype(bf16)
    out_ref[LANES : 2 * LANES, :] = mixed.astype(bf16)
    first = diag.astype(bf16)
    rest = diag - first.astype(f32)
    second = rest.astype(bf16)
    third = (rest - second.astype(f32)).astype(bf16)
    zeros = jnp.zeros((10, LANES), f32)
    tail = jnp.concatenate([part.astype(f32) for part in (first, second, third)] + [zeros], axis=0)
    out_ref[2 * LANES :, :] = tail.astype(bf16)


def sum_packed(refs):
    body = sum(ref[0 : 2 * LANES, :].astype(f32) for ref in refs)
    tail = sum(ref[2 * LANES :, :].astype(f32) for ref in refs)
    diag = tail[0:2] + tail[2:4] + tail[4:6]
    return body[:LANES], body[LANES:], diag


def gram_kernel(view_ref, packed_ref, normed_ref, gram_ref):
    feats = view_ref.shape[1]
    for k in range(feats // WIDE):
        cols = slice(k * WIDE, (k + 1) * WIDE)
        values = view_ref[:, cols].astype(f32)
        mean, inv = scaled(values)
        normed = ((values - mean) * inv).astype(bf16)
        normed_ref[:, cols] = normed
        part = lax.dot_general(normed, normed, (((1,), (1,)), ((), ())), preferred_element_type=f32)
        gram_ref[...] = part if k == 0 else gram_ref[...] + part
    row, col = triangle()
    top, bottom = gram_ref[:LANES, :LANES], gram_ref[LANES:, LANES:]
    diag = jnp.concatenate([total(jnp.where(row == col, part, 0.0)) for part in (top, bottom)], axis=0)
    mixed = jnp.where(row < col, top, jnp.where(row > col, bottom, 0.0))
    store_packed(packed_ref, gram_ref[:LANES, LANES:], mixed, diag)


PACKED = (2 * LANES + 16, LANES)


def gram(view):
    sessions, feats = view.shape
    return pl.pallas_call(
        gram_kernel,
        out_shape=(jax.ShapeDtypeStruct(PACKED, bf16), jax.ShapeDtypeStruct((sessions, feats), bf16)),
        scratch_shapes=[pltpu.VMEM((sessions, sessions), f32)],
        compiler_params=params(),
        name="gram",
    )(view)


def add_kernel(*refs):
    store_packed(refs[-1], *sum_packed(refs[:-1]))


def add_packed(parts):
    return pl.pallas_call(
        add_kernel,
        out_shape=jax.ShapeDtypeStruct(PACKED, bf16),
        compiler_params=params(),
        name="add_packed",
    )(*parts)


def others(packed, axes, size):
    return [packed] + [lax.ppermute(packed, axes, [(i, i ^ k) for i in range(size)]) for k in range(1, size)]


def prepare_kernel(view_ref, other_ref, normed_ref, stats_ref):
    sessions, feats = view_ref.shape
    for k in range(feats // WIDE):
        cols = slice(k * WIDE, (k + 1) * WIDE)
        values = view_ref[:, cols].astype(f32)
        other = other_ref[:, cols].astype(f32)
        mean, inv = scaled(values)
        centered = (values - mean) * inv
        normed = centered.astype(bf16)
        normed_ref[:, cols] = normed
        diagonal = total(normed.astype(f32) * other) / sessions
        rows = [mean, inv, diagonal, total(other), total(other * centered)]
        for r, row in enumerate(rows):
            stats_ref[r : r + 1, cols] = row


def prepare(view, other):
    sessions, feats = view.shape
    return pl.pallas_call(
        prepare_kernel,
        out_shape=(jax.ShapeDtypeStruct((sessions, feats), bf16), jax.ShapeDtypeStruct((8, feats), f32)),
        compiler_params=params(),
        name="prepare",
    )(view, other)


def finish_kernel(x_size, x_ref, p0, p1, p2, p3, view_ref, normed_ref, other_ref, stats_ref, out_ref, high_ref, low_ref, mix_ref, loss_ref):
    sessions, feats = view_ref.shape
    rows = out_ref.shape[1]
    corner, mixed, diag = sum_packed((p0, p1, p2, p3))
    row, col = triangle()
    upper, lower = jnp.where(row < col, mixed, 0.0), jnp.where(row > col, mixed, 0.0)
    top = upper + upper.T + jnp.where(row == col, diag[0:1], 0.0)
    bottom = lower + lower.T + jnp.where(row == col, diag[1:2], 0.0)
    halves = (slice(0, LANES), slice(LANES, 2 * LANES))
    for r, c, part in ((0, 0, top), (0, 1, corner), (1, 0, corner.T), (1, 1, bottom)):
        high = part.astype(bf16)
        high_ref[halves[r], halves[c]] = high
        low_ref[halves[r], halves[c]] = (part - high.astype(f32)).astype(bf16)

    factor = 2.0 * off_weight / sessions
    for k in range(feats // WIDE):
        cols = slice(k * WIDE, (k + 1) * WIDE)
        normed = normed_ref[:, cols]
        mix = jnp.dot(high_ref[...], normed, preferred_element_type=f32)
        mix = mix + jnp.dot(low_ref[...], normed, preferred_element_type=f32)
        mix_ref[...] = mix
        mean, inv, diagonal = (stats_ref[r : r + 1, cols] for r in range(3))
        sum_other, dot_other = (stats_ref[r : r + 1, cols] for r in range(3, 5))
        centered = (view_ref[:, cols].astype(f32) - mean) * inv
        shift = 2.0 * (diagonal - 1.0) - 2.0 * off_weight * diagonal
        sum_all = (factor * total(mix) + shift * sum_other) / sessions
        dot_all = (factor * total(mix * centered) + shift * dot_other) / sessions
        square = total(mix * normed.astype(f32)) / (sessions * sessions)
        loss = (1.0 - diagonal) * (1.0 - diagonal) + off_weight * (square - diagonal * diagonal)
        for yl in range(2):
            for c in range(2):
                begin = pl.multiple_of(((yl * x_size + x_ref[0]) * 2 + c) * rows, rows)
                mine = pl.ds(begin, rows)
                own = (view_ref[mine, cols].astype(f32) - mean) * inv
                grad = factor * mix_ref[mine, :] + shift * other_ref[mine, cols].astype(f32)
                out_ref[yl * 2 + c, :, cols] = (inv * (grad - sum_all - own * dot_all)).astype(bf16)
        for j in range(WIDE // LANES):
            r = k * (WIDE // LANES) + j
            loss_ref[r : r + 1, :] = loss[:, j * LANES : (j + 1) * LANES]
    high = loss_ref[...].astype(bf16)
    low = (loss_ref[...] - high.astype(f32)).astype(bf16)
    for dest in range(4):
        out_ref[dest, :, feats : feats + LANES] = high
        out_ref[dest, :, feats + LANES :] = low


def finish(parts, view, normed, other, stats, x_index, x_size, rows):
    sessions, feats = view.shape
    vmem = pl.BlockSpec(memory_space=pltpu.VMEM)
    return pl.pallas_call(
        functools.partial(finish_kernel, x_size),
        in_specs=[pl.BlockSpec(memory_space=pltpu.SMEM)] + [vmem] * 8,
        out_specs=vmem,
        out_shape=jax.ShapeDtypeStruct((4, rows, feats + 2 * LANES), bf16),
        scratch_shapes=[
            pltpu.VMEM((sessions, sessions), bf16),
            pltpu.VMEM((sessions, sessions), bf16),
            pltpu.VMEM((sessions, WIDE), f32),
            pltpu.VMEM((feats // LANES, LANES), f32),
        ],
        compiler_params=params(),
        name="finish",
    )(x_index, *parts, view, normed, other, stats)


def unpack_kernel(pieces_ref, first_ref, second_ref, loss_ref):
    rows, half = first_ref.shape[0], first_ref.shape[1] // 2
    for yl in range(2):
        cols = slice(yl * half, (yl + 1) * half)
        first_ref[:, cols] = pieces_ref[2 * yl, :, :half].astype(f32)
        second_ref[:, cols] = pieces_ref[2 * yl + 1, :, :half].astype(f32)
        high = pieces_ref[2 * yl, :, half : half + LANES].astype(f32)
        low = pieces_ref[2 * yl, :, half + LANES :].astype(f32)
        loss_ref[yl * rows : (yl + 1) * rows, :] = high + low


def unpack(pieces):
    _, rows, width = pieces.shape
    half = width - 2 * LANES
    grad = jax.ShapeDtypeStruct((rows, 2 * half), f32)
    return pl.pallas_call(
        unpack_kernel,
        out_shape=(grad, grad, jax.ShapeDtypeStruct((2 * rows, LANES), f32)),
        compiler_params=params(),
        name="unpack",
    )(pieces)


def on_device(states, token_ids, crop_start, crop_len, item_weight):
    local_rows = states.shape[0]
    x_size, z_size = lax.axis_size("x"), lax.axis_size("z")
    pooled = pool(states, token_ids, crop_start, crop_len, item_weight, x_size)
    dp_size = 4 * x_size
    half = pooled.shape[-1]
    other_view = lax.all_to_all(
        pooled.reshape(dp_size, local_rows, half), DP, split_axis=0, concat_axis=0, tiled=True
    ).reshape(dp_size * local_rows, half)
    view = lax.ppermute(other_view, "c", [(0, 1), (1, 0)])
    packed, other = gram(other_view)
    normed, stats = prepare(view, other)
    packed = add_packed(others(packed, ("yl", "yh"), 4))
    parts = others(packed, ("z",), z_size)
    x_index = lax.axis_index("x").reshape(1)
    pieces = finish(parts, view, normed, other, stats, x_index, x_size, local_rows)
    pieces = lax.all_to_all(pieces, ("yl", "c"), split_axis=0, concat_axis=0, tiled=True)
    grad_first, grad_second, loss_rows = unpack(pieces)
    return grad_first, grad_second, loss_rows.reshape(-1)


def solution(mesh):
    fine = Mesh(mesh.devices.reshape(2, 4, 2, 2, 4), DP + FEAT)
    placed = (P(DP, None, FEAT), P(DP, None), P(None, DP), P(None, DP), P())
    return jax.shard_map(
        on_device,
        mesh=fine,
        in_specs=placed,
        out_specs=(P(DP, FEAT), P(DP, FEAT), P(FEAT)),
        check_vma=False,
    )
```

```python
import functools

import jax
import jax.numpy as jnp
from jax import lax
from jax.experimental import pallas as pl
from jax.experimental.pallas import tpu as pltpu
from jax.sharding import Mesh
from jax.sharding import PartitionSpec as P

off_weight = 0.0051
eps_norm = 1e-05

f32 = jnp.float32
bf16 = jnp.bfloat16

DP = ("yl", "x", "c")
FEAT = ("yh", "z")
WIDE = 512
POOL_WIDE = 2048
POOL_COPIES = 2
POOL_VMEM = 60
LANES = 128


def iota(shape, dim):
    return lax.broadcasted_iota(jnp.int32, shape, dim)


def params(mib=24):
    return pltpu.CompilerParams(vmem_limit_bytes=mib * 1024 * 1024)


def total(values):
    return jnp.sum(values, axis=0, keepdims=True)


def scaled(values):
    count = values.shape[0]
    mean = total(values) / count
    var = total(values * values) / count - mean * mean
    return mean, lax.rsqrt(var + eps_norm)


def coefficient_rows(ids, start, length, table):
    sessions, tokens = ids.shape
    cols = sessions * tokens
    spread = jnp.where(iota((tokens, cols), 1) % tokens == iota((tokens, cols), 0), 1.0, 0.0).astype(bf16)
    own = iota((sessions, cols), 1) // tokens == iota((sessions, cols), 0)

    def in_line(small):
        rows = jnp.dot(small.astype(f32).astype(bf16), spread, preferred_element_type=f32)
        return total(jnp.where(own, rows, 0.0))

    high, low = in_line(ids // LANES), in_line(ids % LANES)
    place = iota((LANES, cols), 0).astype(f32)
    pick_high = jnp.where(place == high, 1.0, 0.0).astype(bf16)
    first = table.astype(bf16)
    rest = table - first.astype(f32)
    second = rest.astype(bf16)
    third = (rest - second.astype(f32)).astype(bf16)
    found = jnp.zeros((LANES, cols), f32)
    for part in (first, second, third):
        found = found + lax.dot_general(part, pick_high, (((0,), (0,)), ((), ())), preferred_element_type=f32)
    weight = total(jnp.where(place == low, found, 0.0))

    def column(pair):
        spread_rows = jnp.concatenate(
            [jnp.broadcast_to(pair[v : v + 1].astype(f32), (sessions, sessions)) for v in range(2)], axis=0
        )
        square = (2 * sessions, sessions)
        mine = iota(square, 0) % sessions == iota(square, 1)
        return jnp.sum(jnp.where(mine, spread_rows, 0.0), axis=1, keepdims=True)

    first_place, past = column(start), column(start + length)
    shape = (2 * sessions, cols)
    col = iota(shape, 1)
    token = (col % tokens).astype(f32)
    inside = (col // tokens == iota(shape, 0) % sessions) & (token >= first_place) & (token < past)
    masked = jnp.where(inside, weight, 0.0)
    return masked / jnp.sum(masked, axis=1, keepdims=True)


def pool_kernel(
    ids_hbm, start_hbm, len_hbm, table_hbm, states_hbm, out_hbm,
    ids_ref, start_ref, len_ref, table_ref, states_ref, sums_ref, views_ref, small_sem, block_sem, out_sem,
):
    sessions, tokens, feats = states_ref.shape
    pairs = ((ids_hbm, ids_ref), (start_hbm, start_ref), (len_hbm, len_ref), (table_hbm, table_ref))
    small = [pltpu.make_async_copy(src, dst, small_sem.at[i]) for i, (src, dst) in enumerate(pairs)]
    part = sessions // POOL_COPIES
    large = [
        pltpu.make_async_copy(
            states_hbm.at[pl.ds(k * part, part)], states_ref.at[pl.ds(k * part, part)], block_sem.at[k]
        )
        for k in range(POOL_COPIES)
    ]
    for copy in small + large:
        copy.start()
    for copy in small:
        copy.wait()
    coefficients = coefficient_rows(ids_ref[...], start_ref[...], len_ref[...], table_ref[...])
    group = sessions // 2
    half = feats // 2
    out = []
    for g in range(2):
        own = slice(g * group * tokens, (g + 1) * group * tokens)
        rows = [coefficients[v * sessions + g * group : v * sessions + (g + 1) * group, own] for v in range(2)]
        left = jnp.concatenate(rows, axis=0).astype(bf16)
        for copy in large[g * POOL_COPIES // 2 : (g + 1) * POOL_COPIES // 2]:
            copy.wait()
        for k in range(feats // POOL_WIDE):
            cols = slice(k * POOL_WIDE, (k + 1) * POOL_WIDE)
            block = states_ref[g * group : (g + 1) * group, :, cols].reshape(group * tokens, POOL_WIDE)
            views = jnp.dot(left, block, preferred_element_type=f32)
            if g == 0:
                sums_ref[:, cols] = views
                continue
            early = sums_ref[:, cols]
            views_ref[0, :, cols] = jnp.concatenate([early[group:], views[group:]], axis=0).astype(bf16)
            views_ref[1, :, cols] = jnp.concatenate([early[:group], views[:group]], axis=0).astype(bf16)
            yl = cols.start // half
            place = slice(cols.start - yl * half, cols.stop - yl * half)
            for x in range(out_hbm.shape[1]):
                copy = pltpu.make_async_copy(views_ref.at[:, :, cols], out_hbm.at[yl, x, :, :, place], out_sem.at[k, x])
                copy.start()
                out.append(copy)
    for copy in out:
        copy.wait()


def pool(states, token_ids, crop_start, crop_len, item_weight, x_size):
    sessions, tokens, feats = states.shape
    table = item_weight.reshape(-1, LANES)
    small = (token_ids, crop_start, crop_len, table)
    count = feats // POOL_WIDE
    hbm = pl.BlockSpec(memory_space=pltpu.HBM)
    return pl.pallas_call(
        pool_kernel,
        in_specs=[hbm] * 5,
        out_specs=hbm,
        out_shape=jax.ShapeDtypeStruct((2, x_size, 2, sessions, feats // 2), bf16),
        scratch_shapes=[pltpu.VMEM(array.shape, array.dtype) for array in (*small, states)]
        + [
            pltpu.VMEM((sessions, feats), f32),
            pltpu.VMEM((2, sessions, feats), bf16),
            pltpu.SemaphoreType.DMA((len(small),)),
            pltpu.SemaphoreType.DMA((POOL_COPIES,)),
            pltpu.SemaphoreType.DMA((count, x_size)),
        ],
        compiler_params=params(POOL_VMEM),
        name="pool",
    )(*small, states)


def triangle():
    shape = (LANES, LANES)
    return iota(shape, 0), iota(shape, 1)


def store_packed(out_ref, corner, mixed, diag):
    out_ref[0:LANES, :] = corner.astype(bf16)
    out_ref[LANES : 2 * LANES, :] = mixed.astype(bf16)
    first = diag.astype(bf16)
    rest = diag - first.astype(f32)
    second = rest.astype(bf16)
    third = (rest - second.astype(f32)).astype(bf16)
    zeros = jnp.zeros((10, LANES), f32)
    tail = jnp.concatenate([part.astype(f32) for part in (first, second, third)] + [zeros], axis=0)
    out_ref[2 * LANES :, :] = tail.astype(bf16)


def sum_packed(refs):
    body = sum(ref[0 : 2 * LANES, :].astype(f32) for ref in refs)
    tail = sum(ref[2 * LANES :, :].astype(f32) for ref in refs)
    diag = tail[0:2] + tail[2:4] + tail[4:6]
    return body[:LANES], body[LANES:], diag


def gram_kernel(view_ref, packed_ref, normed_ref, gram_ref):
    feats = view_ref.shape[1]
    for k in range(feats // WIDE):
        cols = slice(k * WIDE, (k + 1) * WIDE)
        values = view_ref[:, cols].astype(f32)
        mean, inv = scaled(values)
        normed = ((values - mean) * inv).astype(bf16)
        normed_ref[:, cols] = normed
        part = lax.dot_general(normed, normed, (((1,), (1,)), ((), ())), preferred_element_type=f32)
        gram_ref[...] = part if k == 0 else gram_ref[...] + part
    row, col = triangle()
    top, bottom = gram_ref[:LANES, :LANES], gram_ref[LANES:, LANES:]
    diag = jnp.concatenate([total(jnp.where(row == col, part, 0.0)) for part in (top, bottom)], axis=0)
    mixed = jnp.where(row < col, top, jnp.where(row > col, bottom, 0.0))
    store_packed(packed_ref, gram_ref[:LANES, LANES:], mixed, diag)


PACKED = (2 * LANES + 16, LANES)


def gram(view):
    sessions, feats = view.shape
    return pl.pallas_call(
        gram_kernel,
        out_shape=(jax.ShapeDtypeStruct(PACKED, bf16), jax.ShapeDtypeStruct((sessions, feats), bf16)),
        scratch_shapes=[pltpu.VMEM((sessions, sessions), f32)],
        compiler_params=params(),
        name="gram",
    )(view)


def add_kernel(*refs):
    store_packed(refs[-1], *sum_packed(refs[:-1]))


def add_packed(parts):
    return pl.pallas_call(
        add_kernel,
        out_shape=jax.ShapeDtypeStruct(PACKED, bf16),
        compiler_params=params(),
        name="add_packed",
    )(*parts)


def others(packed, axes, size):
    return [packed] + [lax.ppermute(packed, axes, [(i, i ^ k) for i in range(size)]) for k in range(1, size)]


def prepare_kernel(view_ref, other_ref, normed_ref, stats_ref):
    sessions, feats = view_ref.shape
    for k in range(feats // WIDE):
        cols = slice(k * WIDE, (k + 1) * WIDE)
        values = view_ref[:, cols].astype(f32)
        other = other_ref[:, cols].astype(f32)
        mean, inv = scaled(values)
        centered = (values - mean) * inv
        normed = centered.astype(bf16)
        normed_ref[:, cols] = normed
        diagonal = total(normed.astype(f32) * other) / sessions
        rows = [mean, inv, diagonal, total(other), total(other * centered)]
        for r, row in enumerate(rows):
            stats_ref[r : r + 1, cols] = row


def prepare(view, other):
    sessions, feats = view.shape
    return pl.pallas_call(
        prepare_kernel,
        out_shape=(jax.ShapeDtypeStruct((sessions, feats), bf16), jax.ShapeDtypeStruct((8, feats), f32)),
        compiler_params=params(),
        name="prepare",
    )(view, other)


def finish_kernel(x_size, p0, p1, p2, p3, view_ref, normed_ref, other_ref, stats_ref, *rest):
    sessions, feats = view_ref.shape
    out_refs, (high_ref, low_ref, mix_ref, loss_ref) = rest[:4], rest[4:]
    rows = out_refs[0].shape[0]
    my_yl, my_x, my_c = (lax.axis_index(axis) for axis in DP)
    corner, mixed, diag = sum_packed((p0, p1, p2, p3))
    row, col = triangle()
    upper, lower = jnp.where(row < col, mixed, 0.0), jnp.where(row > col, mixed, 0.0)
    top = upper + upper.T + jnp.where(row == col, diag[0:1], 0.0)
    bottom = lower + lower.T + jnp.where(row == col, diag[1:2], 0.0)
    halves = (slice(0, LANES), slice(LANES, 2 * LANES))
    for r, c, part in ((0, 0, top), (0, 1, corner), (1, 0, corner.T), (1, 1, bottom)):
        high = part.astype(bf16)
        high_ref[halves[r], halves[c]] = high
        low_ref[halves[r], halves[c]] = (part - high.astype(f32)).astype(bf16)

    factor = 2.0 * off_weight / sessions
    for k in range(feats // WIDE):
        cols = slice(k * WIDE, (k + 1) * WIDE)
        normed = normed_ref[:, cols]
        mix = jnp.dot(high_ref[...], normed, preferred_element_type=f32)
        mix = mix + jnp.dot(low_ref[...], normed, preferred_element_type=f32)
        mix_ref[...] = mix
        mean, inv, diagonal = (stats_ref[r : r + 1, cols] for r in range(3))
        sum_other, dot_other = (stats_ref[r : r + 1, cols] for r in range(3, 5))
        centered = (view_ref[:, cols].astype(f32) - mean) * inv
        shift = 2.0 * (diagonal - 1.0) - 2.0 * off_weight * diagonal
        sum_all = (factor * total(mix) + shift * sum_other) / sessions
        dot_all = (factor * total(mix * centered) + shift * dot_other) / sessions
        square = total(mix * normed.astype(f32)) / (sessions * sessions)
        loss = (1.0 - diagonal) * (1.0 - diagonal) + off_weight * (square - diagonal * diagonal)
        for dest, out_ref in enumerate(out_refs):
            chip = (my_yl ^ (dest // 2)) * x_size + my_x
            begin = pl.multiple_of((chip * 2 + (my_c ^ (dest % 2))) * rows, rows)
            mine = pl.ds(begin, rows)
            own = (view_ref[mine, cols].astype(f32) - mean) * inv
            grad = factor * mix_ref[mine, :] + shift * other_ref[mine, cols].astype(f32)
            out_ref[:, cols] = (inv * (grad - sum_all - own * dot_all)).astype(bf16)
        for j in range(WIDE // LANES):
            r = k * (WIDE // LANES) + j
            loss_ref[r : r + 1, :] = loss[:, j * LANES : (j + 1) * LANES]
    high = loss_ref[...].astype(bf16)
    low = (loss_ref[...] - high.astype(f32)).astype(bf16)
    for out_ref in out_refs:
        out_ref[:, feats : feats + LANES] = high
        out_ref[:, feats + LANES :] = low


def finish(parts, view, normed, other, stats, x_size, rows):
    sessions, feats = view.shape
    vmem = pl.BlockSpec(memory_space=pltpu.VMEM)
    return pl.pallas_call(
        functools.partial(finish_kernel, x_size),
        in_specs=[vmem] * 8,
        out_specs=[vmem] * 4,
        out_shape=[jax.ShapeDtypeStruct((rows, feats + 2 * LANES), bf16)] * 4,
        scratch_shapes=[
            pltpu.VMEM((sessions, sessions), bf16),
            pltpu.VMEM((sessions, sessions), bf16),
            pltpu.VMEM((sessions, WIDE), f32),
            pltpu.VMEM((feats // LANES, LANES), f32),
        ],
        compiler_params=params(),
        name="finish",
    )(*parts, view, normed, other, stats)


def unpack_kernel(*refs):
    pieces, (first_ref, second_ref, loss_ref) = refs[:4], refs[4:]
    rows, half = first_ref.shape[0], first_ref.shape[1] // 2
    grads = (first_ref, second_ref)

    def place(my_yl, my_c):
        for source, piece_ref in enumerate(pieces):
            yl, c = my_yl ^ (source // 2), my_c ^ (source % 2)
            grads[c][:, yl * half : (yl + 1) * half] = piece_ref[:, :half].astype(f32)
            if c == 0:
                high, low = piece_ref[:, half : half + LANES], piece_ref[:, half + LANES :]
                loss_ref[yl * rows : (yl + 1) * rows, :] = high.astype(f32) + low.astype(f32)

    here_yl, here_c = lax.axis_index("yl"), lax.axis_index("c")
    for yl in range(2):
        for c in range(2):
            pl.when((here_yl == yl) & (here_c == c))(lambda yl=yl, c=c: place(yl, c))


def unpack(pieces):
    rows, width = pieces[0].shape
    half = width - 2 * LANES
    vmem = pl.BlockSpec(memory_space=pltpu.VMEM)
    grad = jax.ShapeDtypeStruct((rows, 2 * half), f32)
    return pl.pallas_call(
        unpack_kernel,
        in_specs=[vmem] * 4,
        out_shape=(grad, grad, jax.ShapeDtypeStruct((2 * rows, LANES), f32)),
        compiler_params=params(),
        name="unpack",
    )(*pieces)


def on_device(states, token_ids, crop_start, crop_len, item_weight):
    local_rows = states.shape[0]
    x_size, z_size = lax.axis_size("x"), lax.axis_size("z")
    pooled = pool(states, token_ids, crop_start, crop_len, item_weight, x_size)
    dp_size = 4 * x_size
    half = pooled.shape[-1]
    other_view = lax.all_to_all(
        pooled.reshape(dp_size, local_rows, half), DP, split_axis=0, concat_axis=0, tiled=True
    ).reshape(dp_size * local_rows, half)
    packed, other = gram(other_view)
    _, late_view = lax.optimization_barrier((packed, other_view))
    view = lax.ppermute(late_view, "c", [(0, 1), (1, 0)])
    packed = add_packed(others(packed, ("yl", "yh"), 4))
    normed, stats = prepare(view, other)
    parts = others(packed, ("z",), z_size)
    pieces = finish(parts, view, normed, other, stats, x_size, local_rows)
    pieces = [
        piece if k == 0 else lax.ppermute(piece, ("yl", "c"), [(i, i ^ k) for i in range(4)])
        for k, piece in enumerate(pieces)
    ]
    grad_first, grad_second, loss_rows = unpack(pieces)
    return grad_first, grad_second, loss_rows.reshape(-1)


def solution(mesh):
    fine = Mesh(mesh.devices.reshape(2, 4, 2, 2, 4), DP + FEAT)
    placed = (P(DP, None, FEAT), P(DP, None), P(None, DP), P(None, DP), P())
    return jax.shard_map(
        on_device,
        mesh=fine,
        in_specs=placed,
        out_specs=(P(DP, FEAT), P(DP, FEAT), P(FEAT)),
        check_vma=False,
    )
```

```python
import functools

import jax
import jax.numpy as jnp
from jax import lax
from jax.experimental import pallas as pl
from jax.experimental.pallas import tpu as pltpu
from jax.sharding import Mesh
from jax.sharding import PartitionSpec as P

off_weight = 0.0051
eps_norm = 1e-05

f32 = jnp.float32
bf16 = jnp.bfloat16

DP = ("yl", "x", "c")
FEAT = ("yh", "z")
WIDE = 512
POOL_WIDE = 2048
POOL_COPIES = 2
POOL_VMEM = 60
Y_MOVES = ((2, 3), (3, 2), (1, 1))
Z_MOVES = ((1, 3), (3, 1), (2, 2))
LANES = 128


def iota(shape, dim):
    return lax.broadcasted_iota(jnp.int32, shape, dim)


def params(mib=24):
    return pltpu.CompilerParams(vmem_limit_bytes=mib * 1024 * 1024)


def total(values):
    return jnp.sum(values, axis=0, keepdims=True)


def scaled(values):
    count = values.shape[0]
    mean = total(values) / count
    var = total(values * values) / count - mean * mean
    return mean, lax.rsqrt(var + eps_norm)


def coefficient_rows(ids, start, length, table):
    sessions, tokens = ids.shape
    cols = sessions * tokens
    spread = jnp.where(iota((tokens, cols), 1) % tokens == iota((tokens, cols), 0), 1.0, 0.0).astype(bf16)
    own = iota((sessions, cols), 1) // tokens == iota((sessions, cols), 0)

    def in_line(small):
        rows = jnp.dot(small.astype(f32).astype(bf16), spread, preferred_element_type=f32)
        return total(jnp.where(own, rows, 0.0))

    high, low = in_line(ids // LANES), in_line(ids % LANES)
    place = iota((LANES, cols), 0).astype(f32)
    pick_high = jnp.where(place == high, 1.0, 0.0).astype(bf16)
    turned = table.T
    first = turned.astype(bf16)
    rest = turned - first.astype(f32)
    second = rest.astype(bf16)
    third = (rest - second.astype(f32)).astype(bf16)
    found = jnp.zeros((LANES, cols), f32)
    for part in (first, second, third):
        found = found + jnp.dot(part, pick_high, preferred_element_type=f32)
    weight = total(jnp.where(place == low, found, 0.0))

    def column(pair):
        spread_rows = jnp.concatenate(
            [jnp.broadcast_to(pair[v : v + 1].astype(f32), (sessions, sessions)) for v in range(2)], axis=0
        )
        square = (2 * sessions, sessions)
        mine = iota(square, 0) % sessions == iota(square, 1)
        return jnp.sum(jnp.where(mine, spread_rows, 0.0), axis=1, keepdims=True)

    first_place, past = column(start), column(start + length)
    shape = (2 * sessions, cols)
    col = iota(shape, 1)
    token = (col % tokens).astype(f32)
    inside = (col // tokens == iota(shape, 0) % sessions) & (token >= first_place) & (token < past)
    masked = jnp.where(inside, weight, 0.0)
    return masked / jnp.sum(masked, axis=1, keepdims=True)


def pool_kernel(
    ids_hbm, start_hbm, len_hbm, table_hbm, states_hbm, out_hbm,
    ids_ref, start_ref, len_ref, table_ref, states_ref, sums_ref, views_ref, small_sem, block_sem, out_sem,
):
    sessions, tokens, feats = states_ref.shape
    pairs = ((ids_hbm, ids_ref), (start_hbm, start_ref), (len_hbm, len_ref), (table_hbm, table_ref))
    small = [pltpu.make_async_copy(src, dst, small_sem.at[i]) for i, (src, dst) in enumerate(pairs)]
    part = sessions // POOL_COPIES
    large = [
        pltpu.make_async_copy(
            states_hbm.at[pl.ds(k * part, part)], states_ref.at[pl.ds(k * part, part)], block_sem.at[k]
        )
        for k in range(POOL_COPIES)
    ]
    for copy in small + large:
        copy.start()
    for copy in small:
        copy.wait()
    coefficients = coefficient_rows(ids_ref[...], start_ref[...], len_ref[...], table_ref[...])
    group = sessions // 2
    half = feats // 2
    out = []
    for g in range(2):
        own = slice(g * group * tokens, (g + 1) * group * tokens)
        rows = [coefficients[v * sessions + g * group : v * sessions + (g + 1) * group, own] for v in range(2)]
        left = jnp.concatenate(rows, axis=0).astype(bf16)
        for copy in large[g * POOL_COPIES // 2 : (g + 1) * POOL_COPIES // 2]:
            copy.wait()
        for k in range(feats // POOL_WIDE):
            cols = slice(k * POOL_WIDE, (k + 1) * POOL_WIDE)
            block = states_ref[g * group : (g + 1) * group, :, cols].reshape(group * tokens, POOL_WIDE)
            views = jnp.dot(left, block, preferred_element_type=f32)
            if g == 0:
                sums_ref[:, cols] = views
                continue
            early = sums_ref[:, cols]
            views_ref[0, :, cols] = jnp.concatenate([early[group:], views[group:]], axis=0).astype(bf16)
            views_ref[1, :, cols] = jnp.concatenate([early[:group], views[:group]], axis=0).astype(bf16)
            yl = cols.start // half
            place = slice(cols.start - yl * half, cols.stop - yl * half)
            for x in range(out_hbm.shape[1]):
                copy = pltpu.make_async_copy(views_ref.at[:, :, cols], out_hbm.at[yl, x, :, :, place], out_sem.at[k, x])
                copy.start()
                out.append(copy)
    for copy in out:
        copy.wait()


def pool(states, token_ids, crop_start, crop_len, item_weight, x_size):
    sessions, tokens, feats = states.shape
    table = item_weight.reshape(-1, LANES)
    small = (token_ids, crop_start, crop_len, table)
    count = feats // POOL_WIDE
    hbm = pl.BlockSpec(memory_space=pltpu.HBM)
    return pl.pallas_call(
        pool_kernel,
        in_specs=[hbm] * 5,
        out_specs=hbm,
        out_shape=jax.ShapeDtypeStruct((2, x_size, 2, sessions, feats // 2), bf16),
        scratch_shapes=[pltpu.VMEM(array.shape, array.dtype) for array in (*small, states)]
        + [
            pltpu.VMEM((sessions, feats), f32),
            pltpu.VMEM((2, sessions, feats), bf16),
            pltpu.SemaphoreType.DMA((len(small),)),
            pltpu.SemaphoreType.DMA((POOL_COPIES,)),
            pltpu.SemaphoreType.DMA((count, x_size)),
        ],
        compiler_params=params(POOL_VMEM),
        name="pool",
    )(*small, states)


def triangle():
    shape = (LANES, LANES)
    return iota(shape, 0), iota(shape, 1)


def store_packed(out_ref, corner, mixed, diag):
    out_ref[0:LANES, :] = corner.astype(bf16)
    out_ref[LANES : 2 * LANES, :] = mixed.astype(bf16)
    first = diag.astype(bf16)
    rest = diag - first.astype(f32)
    second = rest.astype(bf16)
    third = (rest - second.astype(f32)).astype(bf16)
    zeros = jnp.zeros((10, LANES), f32)
    tail = jnp.concatenate([part.astype(f32) for part in (first, second, third)] + [zeros], axis=0)
    out_ref[2 * LANES :, :] = tail.astype(bf16)


def sum_packed(refs):
    body = sum(ref[0 : 2 * LANES, :].astype(f32) for ref in refs)
    tail = sum(ref[2 * LANES :, :].astype(f32) for ref in refs)
    diag = tail[0:2] + tail[2:4] + tail[4:6]
    return body[:LANES], body[LANES:], diag


def gram_kernel(view_ref, packed_ref, normed_ref, gram_ref):
    feats = view_ref.shape[1]
    for k in range(feats // WIDE):
        cols = slice(k * WIDE, (k + 1) * WIDE)
        values = view_ref[:, cols].astype(f32)
        mean, inv = scaled(values)
        normed = ((values - mean) * inv).astype(bf16)
        normed_ref[:, cols] = normed
        part = lax.dot_general(normed, normed, (((1,), (1,)), ((), ())), preferred_element_type=f32)
        gram_ref[...] = part if k == 0 else gram_ref[...] + part
    row, col = triangle()
    top, bottom = gram_ref[:LANES, :LANES], gram_ref[LANES:, LANES:]
    diag = jnp.concatenate([total(jnp.where(row == col, part, 0.0)) for part in (top, bottom)], axis=0)
    mixed = jnp.where(row < col, top, jnp.where(row > col, bottom, 0.0))
    store_packed(packed_ref, gram_ref[:LANES, LANES:], mixed, diag)


PACKED = (2 * LANES + 16, LANES)


def gram(view):
    sessions, feats = view.shape
    return pl.pallas_call(
        gram_kernel,
        out_shape=(jax.ShapeDtypeStruct(PACKED, bf16), jax.ShapeDtypeStruct((sessions, feats), bf16)),
        scratch_shapes=[pltpu.VMEM((sessions, sessions), f32)],
        compiler_params=params(),
        name="gram",
    )(view)


def add_kernel(*refs):
    store_packed(refs[-1], *sum_packed(refs[:-1]))


def add_packed(parts):
    return pl.pallas_call(
        add_kernel,
        out_shape=jax.ShapeDtypeStruct(PACKED, bf16),
        compiler_params=params(),
        name="add_packed",
    )(*parts)


def others(packed, axes, moves):
    parts = [packed]
    for move in moves:
        pairs = []
        for first in range(2):
            for core in range(2):
                for last in range(2):
                    flip = move[core]
                    pairs.append((first * 4 + core * 2 + last, (first ^ (flip // 2)) * 4 + core * 2 + (last ^ (flip % 2))))
        parts.append(lax.ppermute(packed, axes, pairs))
    return parts


def prepare_kernel(view_ref, other_ref, normed_ref, stats_ref):
    sessions, feats = view_ref.shape
    for k in range(feats // WIDE):
        cols = slice(k * WIDE, (k + 1) * WIDE)
        values = view_ref[:, cols].astype(f32)
        other = other_ref[:, cols].astype(f32)
        mean, inv = scaled(values)
        normed = ((values - mean) * inv).astype(bf16)
        normed_ref[:, cols] = normed
        rows = [inv, total(normed.astype(f32) * other) / sessions, total(other)]
        for r, row in enumerate(rows):
            stats_ref[r : r + 1, cols] = row


def prepare(view, other):
    sessions, feats = view.shape
    return pl.pallas_call(
        prepare_kernel,
        out_shape=(jax.ShapeDtypeStruct((sessions, feats), bf16), jax.ShapeDtypeStruct((8, feats), f32)),
        compiler_params=params(),
        name="prepare",
    )(view, other)


def finish_kernel(x_size, p0, p1, p2, p3, normed_ref, other_ref, stats_ref, *rest):
    sessions, feats = normed_ref.shape
    out_refs, (high_ref, low_ref, mix_ref, loss_ref) = rest[:4], rest[4:]
    rows = out_refs[0].shape[0]
    my_yl, my_x, my_c = (lax.axis_index(axis) for axis in DP)
    corner, mixed, diag = sum_packed((p0, p1, p2, p3))
    row, col = triangle()
    upper, lower = jnp.where(row < col, mixed, 0.0), jnp.where(row > col, mixed, 0.0)
    top = upper + upper.T + jnp.where(row == col, diag[0:1], 0.0)
    bottom = lower + lower.T + jnp.where(row == col, diag[1:2], 0.0)
    halves = (slice(0, LANES), slice(LANES, 2 * LANES))
    for r, c, part in ((0, 0, top), (0, 1, corner), (1, 0, corner.T), (1, 1, bottom)):
        high = part.astype(bf16)
        high_ref[halves[r], halves[c]] = high
        low_ref[halves[r], halves[c]] = (part - high.astype(f32)).astype(bf16)

    factor = 2.0 * off_weight / sessions
    for k in range(feats // WIDE):
        cols = slice(k * WIDE, (k + 1) * WIDE)
        normed = normed_ref[:, cols]
        mix = jnp.dot(high_ref[...], normed, preferred_element_type=f32)
        mix = mix + jnp.dot(low_ref[...], normed, preferred_element_type=f32)
        mix_ref[...] = mix
        inv, diagonal, sum_other = (stats_ref[r : r + 1, cols] for r in range(3))
        shift = 2.0 * (diagonal - 1.0) - 2.0 * off_weight * diagonal
        along = total(mix * normed.astype(f32)) / sessions
        sum_all = (factor * total(mix) + shift * sum_other) / sessions
        dot_all = factor * along + shift * diagonal
        square = along / sessions
        loss = (1.0 - diagonal) * (1.0 - diagonal) + off_weight * (square - diagonal * diagonal)
        for dest, out_ref in enumerate(out_refs):
            chip = (my_yl ^ (dest // 2)) * x_size + my_x
            begin = pl.multiple_of((chip * 2 + (my_c ^ (dest % 2))) * rows, rows)
            mine = pl.ds(begin, rows)
            own = normed_ref[mine, cols].astype(f32)
            grad = factor * mix_ref[mine, :] + shift * other_ref[mine, cols].astype(f32)
            out_ref[:, cols] = (inv * (grad - sum_all - own * dot_all)).astype(bf16)
        for j in range(WIDE // LANES):
            r = k * (WIDE // LANES) + j
            loss_ref[r : r + 1, :] = loss[:, j * LANES : (j + 1) * LANES]
    high = loss_ref[...].astype(bf16)
    low = (loss_ref[...] - high.astype(f32)).astype(bf16)
    for out_ref in out_refs:
        out_ref[:, feats : feats + LANES] = high
        out_ref[:, feats + LANES :] = low


def finish(parts, normed, other, stats, x_size, rows):
    sessions, feats = normed.shape
    vmem = pl.BlockSpec(memory_space=pltpu.VMEM)
    return pl.pallas_call(
        functools.partial(finish_kernel, x_size),
        in_specs=[vmem] * 7,
        out_specs=[vmem] * 4,
        out_shape=[jax.ShapeDtypeStruct((rows, feats + 2 * LANES), bf16)] * 4,
        scratch_shapes=[
            pltpu.VMEM((sessions, sessions), bf16),
            pltpu.VMEM((sessions, sessions), bf16),
            pltpu.VMEM((sessions, WIDE), f32),
            pltpu.VMEM((feats // LANES, LANES), f32),
        ],
        compiler_params=params(),
        name="finish",
    )(*parts, normed, other, stats)


def unpack_kernel(*refs):
    pieces, (first_ref, second_ref, loss_ref) = refs[:4], refs[4:]
    rows, half = first_ref.shape[0], first_ref.shape[1] // 2
    grads = (first_ref, second_ref)

    def place(my_yl, my_c):
        for source, piece_ref in enumerate(pieces):
            yl, c = my_yl ^ (source // 2), my_c ^ (source % 2)
            grads[c][:, yl * half : (yl + 1) * half] = piece_ref[:, :half].astype(f32)
            if c == 0:
                high, low = piece_ref[:, half : half + LANES], piece_ref[:, half + LANES :]
                loss_ref[yl * rows : (yl + 1) * rows, :] = high.astype(f32) + low.astype(f32)

    here_yl, here_c = lax.axis_index("yl"), lax.axis_index("c")
    for yl in range(2):
        for c in range(2):
            pl.when((here_yl == yl) & (here_c == c))(lambda yl=yl, c=c: place(yl, c))


def unpack(pieces):
    rows, width = pieces[0].shape
    half = width - 2 * LANES
    vmem = pl.BlockSpec(memory_space=pltpu.VMEM)
    grad = jax.ShapeDtypeStruct((rows, 2 * half), f32)
    return pl.pallas_call(
        unpack_kernel,
        in_specs=[vmem] * 4,
        out_shape=(grad, grad, jax.ShapeDtypeStruct((2 * rows, LANES), f32)),
        compiler_params=params(),
        name="unpack",
    )(*pieces)


def on_device(states, token_ids, crop_start, crop_len, item_weight):
    local_rows = states.shape[0]
    x_size = lax.axis_size("x")
    pooled = pool(states, token_ids, crop_start, crop_len, item_weight, x_size)
    dp_size = 4 * x_size
    half = pooled.shape[-1]
    other_view = lax.all_to_all(
        pooled.reshape(dp_size, local_rows, half), DP, split_axis=0, concat_axis=0, tiled=True
    ).reshape(dp_size * local_rows, half)
    packed, other = gram(other_view)
    _, late_view = lax.optimization_barrier((packed, other_view))
    view = lax.ppermute(late_view, "c", [(0, 1), (1, 0)])
    packed = add_packed(others(packed, ("yl", "c", "yh"), Y_MOVES))
    normed, stats = prepare(view, other)
    parts = [packed] + [
        lax.ppermute(packed, ("c", "z"), [(c * 4 + z, c * 4 + (z ^ move[c])) for c in range(2) for z in range(4)])
        for move in Z_MOVES
    ]
    pieces = finish(parts, normed, other, stats, x_size, local_rows)
    far = [lax.ppermute(pieces[k], ("yl", "c"), [(i, i ^ k) for i in range(4)]) for k in (2, 3, 1)]
    pieces = [pieces[0], far[2], far[0], far[1]]
    grad_first, grad_second, loss_rows = unpack(pieces)
    return grad_first, grad_second, loss_rows.reshape(-1)


def solution(mesh):
    fine = Mesh(mesh.devices.reshape(2, 4, 2, 2, 4), DP + FEAT)
    placed = (P(DP, None, FEAT), P(DP, None), P(None, DP), P(None, DP), P())
    return jax.shard_map(
        on_device,
        mesh=fine,
        in_specs=placed,
        out_specs=(P(DP, FEAT), P(DP, FEAT), P(FEAT)),
        check_vma=False,
    )
```

```python
import functools

import jax
import jax.numpy as jnp
from jax import lax
from jax.experimental import pallas as pl
from jax.experimental.pallas import tpu as pltpu
from jax.sharding import Mesh
from jax.sharding import PartitionSpec as P

off_weight = 0.0051
eps_norm = 1e-05

f32 = jnp.float32
bf16 = jnp.bfloat16

DP = ("yl", "x", "c")
FEAT = ("yh", "z")
WIDE = 512
POOL_WIDE = 2048
POOL_COPIES = 2
POOL_VMEM = 60
Y_MOVES = ((2, 3), (3, 2), (1, 1))
Z_MOVES = ((1, 3), (3, 1), (2, 2))
LANES = 128


def iota(shape, dim):
    return lax.broadcasted_iota(jnp.int32, shape, dim)


def params(mib=24):
    return pltpu.CompilerParams(vmem_limit_bytes=mib * 1024 * 1024)


def total(values):
    return jnp.sum(values, axis=0, keepdims=True)


def scaled(values):
    count = values.shape[0]
    mean = total(values) / count
    var = total(values * values) / count - mean * mean
    return mean, lax.rsqrt(var + eps_norm)


def coefficient_rows(ids, start, length, table):
    sessions, tokens = ids.shape
    cols = sessions * tokens
    spread = jnp.where(iota((tokens, cols), 1) % tokens == iota((tokens, cols), 0), 1.0, 0.0).astype(bf16)
    own = iota((sessions, cols), 1) // tokens == iota((sessions, cols), 0)

    def in_line(small):
        rows = jnp.dot(small.astype(f32).astype(bf16), spread, preferred_element_type=f32)
        return total(jnp.where(own, rows, 0.0))

    high, low = in_line(ids // LANES), in_line(ids % LANES)
    place = iota((LANES, cols), 0).astype(f32)
    pick_high = jnp.where(place == high, 1.0, 0.0).astype(bf16)
    first = table.astype(bf16)
    rest = table - first.astype(f32)
    second = rest.astype(bf16)
    third = (rest - second.astype(f32)).astype(bf16)
    found = jnp.zeros((LANES, cols), f32)
    for part in (first, second, third):
        found = found + lax.dot_general(part, pick_high, (((0,), (0,)), ((), ())), preferred_element_type=f32)
    weight = total(jnp.where(place == low, found, 0.0))

    def column(pair):
        spread_rows = jnp.concatenate(
            [jnp.broadcast_to(pair[v : v + 1].astype(f32), (sessions, sessions)) for v in range(2)], axis=0
        )
        square = (2 * sessions, sessions)
        mine = iota(square, 0) % sessions == iota(square, 1)
        return jnp.sum(jnp.where(mine, spread_rows, 0.0), axis=1, keepdims=True)

    first_place, past = column(start), column(start + length)
    shape = (2 * sessions, cols)
    col = iota(shape, 1)
    token = (col % tokens).astype(f32)
    inside = (col // tokens == iota(shape, 0) % sessions) & (token >= first_place) & (token < past)
    masked = jnp.where(inside, weight, 0.0)
    return masked / jnp.sum(masked, axis=1, keepdims=True)


def pool_kernel(
    ids_hbm, start_hbm, len_hbm, table_hbm, states_hbm, out_hbm,
    ids_ref, start_ref, len_ref, table_ref, states_ref, sums_ref, views_ref, small_sem, block_sem, out_sem,
):
    sessions, tokens, feats = states_ref.shape
    pairs = ((ids_hbm, ids_ref), (start_hbm, start_ref), (len_hbm, len_ref), (table_hbm, table_ref))
    small = [pltpu.make_async_copy(src, dst, small_sem.at[i]) for i, (src, dst) in enumerate(pairs)]
    part = sessions // POOL_COPIES
    large = [
        pltpu.make_async_copy(
            states_hbm.at[pl.ds(k * part, part)], states_ref.at[pl.ds(k * part, part)], block_sem.at[k]
        )
        for k in range(POOL_COPIES)
    ]
    for copy in small + large:
        copy.start()
    for copy in small:
        copy.wait()
    coefficients = coefficient_rows(ids_ref[...], start_ref[...], len_ref[...], table_ref[...])
    group = sessions // 2
    half = feats // 2
    out = []
    for g in range(2):
        own = slice(g * group * tokens, (g + 1) * group * tokens)
        rows = [coefficients[v * sessions + g * group : v * sessions + (g + 1) * group, own] for v in range(2)]
        left = jnp.concatenate(rows, axis=0).astype(bf16)
        for copy in large[g * POOL_COPIES // 2 : (g + 1) * POOL_COPIES // 2]:
            copy.wait()
        for k in range(feats // POOL_WIDE):
            cols = slice(k * POOL_WIDE, (k + 1) * POOL_WIDE)
            block = states_ref[g * group : (g + 1) * group, :, cols].reshape(group * tokens, POOL_WIDE)
            views = jnp.dot(left, block, preferred_element_type=f32)
            if g == 0:
                sums_ref[:, cols] = views
                continue
            early = sums_ref[:, cols]
            views_ref[0, :, cols] = jnp.concatenate([early[group:], views[group:]], axis=0).astype(bf16)
            views_ref[1, :, cols] = jnp.concatenate([early[:group], views[:group]], axis=0).astype(bf16)
            yl = cols.start // half
            place = slice(cols.start - yl * half, cols.stop - yl * half)
            for x in range(out_hbm.shape[1]):
                copy = pltpu.make_async_copy(views_ref.at[:, :, cols], out_hbm.at[yl, x, :, :, place], out_sem.at[k, x])
                copy.start()
                out.append(copy)
    for copy in out:
        copy.wait()


def pool(states, token_ids, crop_start, crop_len, item_weight, x_size):
    sessions, tokens, feats = states.shape
    table = item_weight.reshape(-1, LANES)
    small = (token_ids, crop_start, crop_len, table)
    count = feats // POOL_WIDE
    hbm = pl.BlockSpec(memory_space=pltpu.HBM)
    return pl.pallas_call(
        pool_kernel,
        in_specs=[hbm] * 5,
        out_specs=hbm,
        out_shape=jax.ShapeDtypeStruct((2, x_size, 2, sessions, feats // 2), bf16),
        scratch_shapes=[pltpu.VMEM(array.shape, array.dtype) for array in (*small, states)]
        + [
            pltpu.VMEM((sessions, feats), f32),
            pltpu.VMEM((2, sessions, feats), bf16),
            pltpu.SemaphoreType.DMA((len(small),)),
            pltpu.SemaphoreType.DMA((POOL_COPIES,)),
            pltpu.SemaphoreType.DMA((count, x_size)),
        ],
        compiler_params=params(POOL_VMEM),
        name="pool",
    )(*small, states)


def triangle():
    shape = (LANES, LANES)
    return iota(shape, 0), iota(shape, 1)


def store_packed(out_ref, corner, mixed, diag):
    out_ref[0:LANES, :] = corner.astype(bf16)
    out_ref[LANES : 2 * LANES, :] = mixed.astype(bf16)
    first = diag.astype(bf16)
    rest = diag - first.astype(f32)
    second = rest.astype(bf16)
    third = (rest - second.astype(f32)).astype(bf16)
    zeros = jnp.zeros((10, LANES), f32)
    tail = jnp.concatenate([part.astype(f32) for part in (first, second, third)] + [zeros], axis=0)
    out_ref[2 * LANES :, :] = tail.astype(bf16)


def sum_packed(refs):
    body = sum(ref[0 : 2 * LANES, :].astype(f32) for ref in refs)
    tail = sum(ref[2 * LANES :, :].astype(f32) for ref in refs)
    diag = tail[0:2] + tail[2:4] + tail[4:6]
    return body[:LANES], body[LANES:], diag


def gram_kernel(view_ref, packed_ref, normed_ref, gram_ref):
    feats = view_ref.shape[1]
    for k in range(feats // WIDE):
        cols = slice(k * WIDE, (k + 1) * WIDE)
        values = view_ref[:, cols].astype(f32)
        mean, inv = scaled(values)
        normed = ((values - mean) * inv).astype(bf16)
        normed_ref[:, cols] = normed
        part = lax.dot_general(normed, normed, (((1,), (1,)), ((), ())), preferred_element_type=f32)
        gram_ref[...] = part if k == 0 else gram_ref[...] + part
    row, col = triangle()
    top, bottom = gram_ref[:LANES, :LANES], gram_ref[LANES:, LANES:]
    diag = jnp.concatenate([total(jnp.where(row == col, part, 0.0)) for part in (top, bottom)], axis=0)
    mixed = jnp.where(row < col, top, jnp.where(row > col, bottom, 0.0))
    store_packed(packed_ref, gram_ref[:LANES, LANES:], mixed, diag)


PACKED = (2 * LANES + 16, LANES)


def gram(view):
    sessions, feats = view.shape
    return pl.pallas_call(
        gram_kernel,
        out_shape=(jax.ShapeDtypeStruct(PACKED, bf16), jax.ShapeDtypeStruct((sessions, feats), bf16)),
        scratch_shapes=[pltpu.VMEM((sessions, sessions), f32)],
        compiler_params=params(),
        name="gram",
    )(view)


def add_kernel(*refs):
    store_packed(refs[-1], *sum_packed(refs[:-1]))


def add_packed(parts):
    return pl.pallas_call(
        add_kernel,
        out_shape=jax.ShapeDtypeStruct(PACKED, bf16),
        compiler_params=params(),
        name="add_packed",
    )(*parts)


def others(packed, axes, moves):
    parts = [packed]
    for move in moves:
        pairs = []
        for first in range(2):
            for core in range(2):
                for last in range(2):
                    flip = move[core]
                    pairs.append((first * 4 + core * 2 + last, (first ^ (flip // 2)) * 4 + core * 2 + (last ^ (flip % 2))))
        parts.append(lax.ppermute(packed, axes, pairs))
    return parts


def prepare_kernel(view_ref, other_ref, centered_ref, normed_ref, stats_ref):
    sessions, feats = view_ref.shape
    for k in range(feats // WIDE):
        cols = slice(k * WIDE, (k + 1) * WIDE)
        values = view_ref[:, cols].astype(f32)
        other = other_ref[:, cols].astype(f32)
        mean, inv = scaled(values)
        centered = (values - mean) * inv
        normed = centered.astype(bf16)
        centered_ref[:, cols] = centered
        normed_ref[:, cols] = normed
        diagonal = total(normed.astype(f32) * other) / sessions
        rows = [inv, diagonal, total(other) / sessions, total(other * centered) / sessions]
        for r, row in enumerate(rows):
            stats_ref[r : r + 1, cols] = row


def prepare(view, other):
    sessions, feats = view.shape
    return pl.pallas_call(
        prepare_kernel,
        out_shape=(
            jax.ShapeDtypeStruct((sessions, feats), f32),
            jax.ShapeDtypeStruct((sessions, feats), bf16),
            jax.ShapeDtypeStruct((8, feats), f32),
        ),
        compiler_params=params(),
        name="prepare",
    )(view, other)


def finish_kernel(x_size, p0, p1, p2, p3, centered_ref, normed_ref, other_ref, stats_ref, *rest):
    sessions, feats = centered_ref.shape
    out_refs, (high_ref, low_ref, mix_ref, loss_ref) = rest[:4], rest[4:]
    rows = out_refs[0].shape[0]
    my_yl, my_x, my_c = (lax.axis_index(axis) for axis in DP)
    corner, mixed, diag = sum_packed((p0, p1, p2, p3))
    row, col = triangle()
    upper, lower = jnp.where(row < col, mixed, 0.0), jnp.where(row > col, mixed, 0.0)
    top = upper + upper.T + jnp.where(row == col, diag[0:1], 0.0)
    bottom = lower + lower.T + jnp.where(row == col, diag[1:2], 0.0)
    halves = (slice(0, LANES), slice(LANES, 2 * LANES))
    for r, c, part in ((0, 0, top), (0, 1, corner), (1, 0, corner.T), (1, 1, bottom)):
        high = part.astype(bf16)
        high_ref[halves[r], halves[c]] = high
        low_ref[halves[r], halves[c]] = (part - high.astype(f32)).astype(bf16)

    factor = 2.0 * off_weight / sessions
    for k in range(feats // WIDE):
        cols = slice(k * WIDE, (k + 1) * WIDE)
        normed = normed_ref[:, cols]
        mix = jnp.dot(high_ref[...], normed, preferred_element_type=f32)
        mix = mix + jnp.dot(low_ref[...], normed, preferred_element_type=f32)
        mix_ref[...] = mix
        inv, diagonal, mean_other, dot_other = (stats_ref[r : r + 1, cols] for r in range(4))
        shift = 2.0 * (diagonal - 1.0) - 2.0 * off_weight * diagonal
        along = total(mix * centered_ref[:, cols]) / sessions
        mean_all = factor / sessions * total(mix) + shift * mean_other
        dot_all = factor * along + shift * dot_other
        square = along / sessions
        loss = (1.0 - diagonal) * (1.0 - diagonal) + off_weight * (square - diagonal * diagonal)
        for dest, out_ref in enumerate(out_refs):
            chip = (my_yl ^ (dest // 2)) * x_size + my_x
            begin = pl.multiple_of((chip * 2 + (my_c ^ (dest % 2))) * rows, rows)
            mine = pl.ds(begin, rows)
            grad = factor * mix_ref[mine, :] + shift * other_ref[mine, cols].astype(f32)
            out_ref[:, cols] = (inv * (grad - mean_all - centered_ref[mine, cols] * dot_all)).astype(bf16)
        for j in range(WIDE // LANES):
            r = k * (WIDE // LANES) + j
            loss_ref[r : r + 1, :] = loss[:, j * LANES : (j + 1) * LANES]
    high = loss_ref[...].astype(bf16)
    low = (loss_ref[...] - high.astype(f32)).astype(bf16)
    for out_ref in out_refs:
        out_ref[:, feats : feats + LANES] = high
        out_ref[:, feats + LANES :] = low


def finish(parts, centered, normed, other, stats, x_size, rows):
    sessions, feats = centered.shape
    vmem = pl.BlockSpec(memory_space=pltpu.VMEM)
    return pl.pallas_call(
        functools.partial(finish_kernel, x_size),
        in_specs=[vmem] * 8,
        out_specs=[vmem] * 4,
        out_shape=[jax.ShapeDtypeStruct((rows, feats + 2 * LANES), bf16)] * 4,
        scratch_shapes=[
            pltpu.VMEM((sessions, sessions), bf16),
            pltpu.VMEM((sessions, sessions), bf16),
            pltpu.VMEM((sessions, WIDE), f32),
            pltpu.VMEM((feats // LANES, LANES), f32),
        ],
        compiler_params=params(),
        name="finish",
    )(*parts, centered, normed, other, stats)


def unpack_kernel(*refs):
    pieces, (first_ref, second_ref, loss_ref) = refs[:4], refs[4:]
    rows, half = first_ref.shape[0], first_ref.shape[1] // 2
    grads = (first_ref, second_ref)

    def place(my_yl, my_c):
        for source, piece_ref in enumerate(pieces):
            yl, c = my_yl ^ (source // 2), my_c ^ (source % 2)
            grads[c][:, yl * half : (yl + 1) * half] = piece_ref[:, :half].astype(f32)
            if c == 0:
                high, low = piece_ref[:, half : half + LANES], piece_ref[:, half + LANES :]
                loss_ref[yl * rows : (yl + 1) * rows, :] = high.astype(f32) + low.astype(f32)

    here_yl, here_c = lax.axis_index("yl"), lax.axis_index("c")
    for yl in range(2):
        for c in range(2):
            pl.when((here_yl == yl) & (here_c == c))(lambda yl=yl, c=c: place(yl, c))


def unpack(pieces):
    rows, width = pieces[0].shape
    half = width - 2 * LANES
    vmem = pl.BlockSpec(memory_space=pltpu.VMEM)
    grad = jax.ShapeDtypeStruct((rows, 2 * half), f32)
    return pl.pallas_call(
        unpack_kernel,
        in_specs=[vmem] * 4,
        out_shape=(grad, grad, jax.ShapeDtypeStruct((2 * rows, LANES), f32)),
        compiler_params=params(),
        name="unpack",
    )(*pieces)


def on_device(states, token_ids, crop_start, crop_len, item_weight):
    local_rows = states.shape[0]
    x_size = lax.axis_size("x")
    pooled = pool(states, token_ids, crop_start, crop_len, item_weight, x_size)
    dp_size = 4 * x_size
    half = pooled.shape[-1]
    other_view = lax.all_to_all(
        pooled.reshape(dp_size, local_rows, half), DP, split_axis=0, concat_axis=0, tiled=True
    ).reshape(dp_size * local_rows, half)
    packed, other = gram(other_view)
    _, late_view = lax.optimization_barrier((packed, other_view))
    view = lax.ppermute(late_view, "c", [(0, 1), (1, 0)])
    packed = add_packed(others(packed, ("yl", "c", "yh"), Y_MOVES))
    centered, normed, stats = prepare(view, other)
    parts = [packed] + [
        lax.ppermute(packed, ("c", "z"), [(c * 4 + z, c * 4 + (z ^ move[c])) for c in range(2) for z in range(4)])
        for move in Z_MOVES
    ]
    pieces = finish(parts, centered, normed, other, stats, x_size, local_rows)
    far = [lax.ppermute(pieces[k], ("yl", "c"), [(i, i ^ k) for i in range(4)]) for k in (2, 3, 1)]
    pieces = [pieces[0], far[2], far[0], far[1]]
    grad_first, grad_second, loss_rows = unpack(pieces)
    return grad_first, grad_second, loss_rows.reshape(-1)


def solution(mesh):
    fine = Mesh(mesh.devices.reshape(2, 4, 2, 2, 4), DP + FEAT)
    placed = (P(DP, None, FEAT), P(DP, None), P(None, DP), P(None, DP), P())
    return jax.shard_map(
        on_device,
        mesh=fine,
        in_specs=placed,
        out_specs=(P(DP, FEAT), P(DP, FEAT), P(FEAT)),
        check_vma=False,
    )
```

```python
import functools

import jax
import jax.numpy as jnp
from jax import lax
from jax.experimental import pallas as pl
from jax.experimental.pallas import tpu as pltpu
from jax.sharding import Mesh
from jax.sharding import PartitionSpec as P

off_weight = 0.0051
eps_norm = 1e-05

f32 = jnp.float32
bf16 = jnp.bfloat16

DP = ("yl", "x", "c")
FEAT = ("yh", "z")
CHIPS = ("yl", "x")
WIDE = 512
POOL_WIDE = 2048
POOL_COPIES = 2
CHIP_ORDER = (7, 6, 5, 2, 3, 1, 4)
POOL_VMEM = 60
Y_MOVES = ((2, 3), (3, 2), (1, 1))
Z_MOVES = ((1, 3), (3, 1), (2, 2))
LANES = 128


def iota(shape, dim):
    return lax.broadcasted_iota(jnp.int32, shape, dim)


def params(mib=24):
    return pltpu.CompilerParams(vmem_limit_bytes=mib * 1024 * 1024)


def total(values):
    return jnp.sum(values, axis=0, keepdims=True)


def scaled(values):
    count = values.shape[0]
    mean = total(values) / count
    var = total(values * values) / count - mean * mean
    return mean, lax.rsqrt(var + eps_norm)


def coefficient_rows(ids, start, length, table, in_order):
    sessions, tokens = ids.shape
    cols = sessions * tokens
    spread = jnp.where(iota((tokens, cols), 1) % tokens == iota((tokens, cols), 0), 1.0, 0.0).astype(bf16)
    own = iota((sessions, cols), 1) // tokens == iota((sessions, cols), 0)

    def in_line(small):
        rows = jnp.dot(small.astype(f32).astype(bf16), spread, preferred_element_type=f32)
        return total(jnp.where(own, rows, 0.0))

    high, low = in_line(ids // LANES), in_line(ids % LANES)
    place = iota((LANES, cols), 0).astype(f32)
    pick_high = jnp.where(place == high, 1.0, 0.0).astype(bf16)
    first = table.astype(bf16)
    rest = table - first.astype(f32)
    second = rest.astype(bf16)
    third = (rest - second.astype(f32)).astype(bf16)
    found = jnp.zeros((LANES, cols), f32)
    for part in (first, second, third):
        found = found + lax.dot_general(part, pick_high, (((0,), (0,)), ((), ())), preferred_element_type=f32)
    weight = total(jnp.where(place == low, found, 0.0))

    def column(pair):
        first, second = pair[0:1].astype(f32), pair[1:2].astype(f32)
        ordered = (jnp.where(in_order, first, second), jnp.where(in_order, second, first))
        spread_rows = jnp.concatenate([jnp.broadcast_to(row, (sessions, sessions)) for row in ordered], axis=0)
        square = (2 * sessions, sessions)
        mine = iota(square, 0) % sessions == iota(square, 1)
        return jnp.sum(jnp.where(mine, spread_rows, 0.0), axis=1, keepdims=True)

    first_place, past = column(start), column(start + length)
    shape = (2 * sessions, cols)
    col = iota(shape, 1)
    token = (col % tokens).astype(f32)
    inside = (col // tokens == iota(shape, 0) % sessions) & (token >= first_place) & (token < past)
    masked = jnp.where(inside, weight, 0.0)
    return masked / jnp.sum(masked, axis=1, keepdims=True)


def pool_kernel(
    ids_hbm, start_hbm, len_hbm, table_hbm, states_hbm, keep_ref, send_ref,
    ids_ref, start_ref, len_ref, table_ref, states_ref, sums_ref, small_sem, block_sem,
):
    sessions, tokens, feats = states_ref.shape
    pairs = ((ids_hbm, ids_ref), (start_hbm, start_ref), (len_hbm, len_ref), (table_hbm, table_ref))
    small = [pltpu.make_async_copy(src, dst, small_sem.at[i]) for i, (src, dst) in enumerate(pairs)]
    part = sessions // POOL_COPIES
    large = [
        pltpu.make_async_copy(
            states_hbm.at[pl.ds(k * part, part)], states_ref.at[pl.ds(k * part, part)], block_sem.at[k]
        )
        for k in range(POOL_COPIES)
    ]
    for copy in small + large:
        copy.start()
    for copy in small:
        copy.wait()
    coefficients = coefficient_rows(
        ids_ref[...], start_ref[...], len_ref[...], table_ref[...], lax.axis_index("c") == 1
    )
    group = sessions // 2
    for g in range(2):
        own = slice(g * group * tokens, (g + 1) * group * tokens)
        rows = [coefficients[v * sessions + g * group : v * sessions + (g + 1) * group, own] for v in range(2)]
        left = jnp.concatenate(rows, axis=0).astype(bf16)
        for copy in large[g * POOL_COPIES // 2 : (g + 1) * POOL_COPIES // 2]:
            copy.wait()
        for k in range(feats // POOL_WIDE):
            cols = slice(k * POOL_WIDE, (k + 1) * POOL_WIDE)
            block = states_ref[g * group : (g + 1) * group, :, cols].reshape(group * tokens, POOL_WIDE)
            views = jnp.dot(left, block, preferred_element_type=f32)
            if g == 0:
                sums_ref[:, cols] = views
                continue
            early = sums_ref[:, cols]
            for v, out_ref in enumerate((keep_ref, send_ref)):
                rows = slice(v * group, (v + 1) * group)
                out_ref[:, cols] = jnp.concatenate([early[rows], views[rows]], axis=0).astype(bf16)


def pool(states, token_ids, crop_start, crop_len, item_weight):
    sessions, tokens, feats = states.shape
    table = item_weight.reshape(-1, LANES)
    small = (token_ids, crop_start, crop_len, table)
    hbm, vmem = pl.BlockSpec(memory_space=pltpu.HBM), pl.BlockSpec(memory_space=pltpu.VMEM)
    return pl.pallas_call(
        pool_kernel,
        in_specs=[hbm] * 5,
        out_specs=(vmem, vmem),
        out_shape=[jax.ShapeDtypeStruct((sessions, feats), bf16)] * 2,
        scratch_shapes=[pltpu.VMEM(array.shape, array.dtype) for array in (*small, states)]
        + [
            pltpu.VMEM((sessions, feats), f32),
            pltpu.SemaphoreType.DMA((len(small),)),
            pltpu.SemaphoreType.DMA((POOL_COPIES,)),
        ],
        compiler_params=params(POOL_VMEM),
        name="pool",
    )(*small, states)


def split_kernel(mine_ref, near_ref, away_ref):
    half = near_ref.shape[1]
    yl = lax.axis_index("yl")
    for k, out_ref in enumerate((near_ref, away_ref)):
        out_ref[...] = mine_ref[:, pl.ds(pl.multiple_of((yl ^ k) * half, half), half)]


def split(mine):
    rows, feats = mine.shape
    return pl.pallas_call(
        split_kernel,
        out_shape=[jax.ShapeDtypeStruct((rows, feats // 2), bf16)] * 2,
        compiler_params=params(),
        name="split",
    )(mine)


def collect_kernel(mine_near_ref, mine_away_ref, far_ref, near_ref, away_ref):
    rows, half = mine_near_ref.shape
    yl, c = lax.axis_index("yl"), lax.axis_index("c")
    for k, (mine_ref, out_ref) in enumerate(((mine_near_ref, near_ref), (mine_away_ref, away_ref))):
        cols = pl.ds(pl.multiple_of((yl ^ k) * half, half), half)
        out_ref[pl.ds(pl.multiple_of(c * rows, rows), rows), :] = mine_ref[...]
        out_ref[pl.ds(pl.multiple_of((1 - c) * rows, rows), rows), :] = far_ref[:, cols]


def collect(mine_near, mine_away, far):
    rows, half = mine_near.shape
    return pl.pallas_call(
        collect_kernel,
        out_shape=[jax.ShapeDtypeStruct((2 * rows, half), bf16)] * 2,
        compiler_params=params(),
        name="collect",
    )(mine_near, mine_away, far)


def triangle():
    shape = (LANES, LANES)
    return iota(shape, 0), iota(shape, 1)


def store_packed(out_ref, corner, mixed, diag):
    out_ref[0:LANES, :] = corner.astype(bf16)
    out_ref[LANES : 2 * LANES, :] = mixed.astype(bf16)
    first = diag.astype(bf16)
    rest = diag - first.astype(f32)
    second = rest.astype(bf16)
    third = (rest - second.astype(f32)).astype(bf16)
    zeros = jnp.zeros((10, LANES), f32)
    tail = jnp.concatenate([part.astype(f32) for part in (first, second, third)] + [zeros], axis=0)
    out_ref[2 * LANES :, :] = tail.astype(bf16)


def sum_packed(refs):
    body = sum(ref[0 : 2 * LANES, :].astype(f32) for ref in refs)
    tail = sum(ref[2 * LANES :, :].astype(f32) for ref in refs)
    diag = tail[0:2] + tail[2:4] + tail[4:6]
    return body[:LANES], body[LANES:], diag


def gram_kernel(order, *refs):
    block_refs, (packed_ref, normed_ref, view_ref, gram_ref) = refs[: len(order)], refs[len(order) :]
    rows, feats = block_refs[0].shape
    chip = lax.axis_index(CHIPS)
    for k, block_ref in zip(order, block_refs, strict=True):
        view_ref[pl.ds(pl.multiple_of((chip ^ k) * rows, rows), rows), :] = block_ref[...]
    for k in range(feats // WIDE):
        cols = slice(k * WIDE, (k + 1) * WIDE)
        values = view_ref[:, cols].astype(f32)
        mean, inv = scaled(values)
        normed = ((values - mean) * inv).astype(bf16)
        normed_ref[:, cols] = normed
        part = lax.dot_general(normed, normed, (((1,), (1,)), ((), ())), preferred_element_type=f32)
        gram_ref[...] = part if k == 0 else gram_ref[...] + part
    row, col = triangle()
    top, bottom = gram_ref[:LANES, :LANES], gram_ref[LANES:, LANES:]
    diag = jnp.concatenate([total(jnp.where(row == col, part, 0.0)) for part in (top, bottom)], axis=0)
    mixed = jnp.where(row < col, top, jnp.where(row > col, bottom, 0.0))
    store_packed(packed_ref, gram_ref[:LANES, LANES:], mixed, diag)


PACKED = (2 * LANES + 16, LANES)


def gram(order, blocks):
    rows, feats = blocks[0].shape
    sessions = len(blocks) * rows
    whole = jax.ShapeDtypeStruct((sessions, feats), bf16)
    return pl.pallas_call(
        functools.partial(gram_kernel, order),
        out_shape=(jax.ShapeDtypeStruct(PACKED, bf16), whole, whole),
        scratch_shapes=[pltpu.VMEM((sessions, sessions), f32)],
        compiler_params=params(),
        name="gram",
    )(*blocks)


def add_kernel(*refs):
    store_packed(refs[-1], *sum_packed(refs[:-1]))


def add_packed(parts):
    return pl.pallas_call(
        add_kernel,
        out_shape=jax.ShapeDtypeStruct(PACKED, bf16),
        compiler_params=params(),
        name="add_packed",
    )(*parts)


def others(packed, axes, moves):
    parts = [packed]
    for move in moves:
        pairs = []
        for first in range(2):
            for core in range(2):
                for last in range(2):
                    flip = move[core]
                    pairs.append((first * 4 + core * 2 + last, (first ^ (flip // 2)) * 4 + core * 2 + (last ^ (flip % 2))))
        parts.append(lax.ppermute(packed, axes, pairs))
    return parts


def prepare_kernel(view_ref, other_ref, centered_ref, normed_ref, stats_ref):
    sessions, feats = view_ref.shape
    for k in range(feats // WIDE):
        cols = slice(k * WIDE, (k + 1) * WIDE)
        values = view_ref[:, cols].astype(f32)
        other = other_ref[:, cols].astype(f32)
        mean, inv = scaled(values)
        centered = (values - mean) * inv
        normed = centered.astype(bf16)
        centered_ref[:, cols] = centered
        normed_ref[:, cols] = normed
        diagonal = total(normed.astype(f32) * other) / sessions
        rows = [inv, diagonal, total(other) / sessions, total(other * centered) / sessions]
        for r, row in enumerate(rows):
            stats_ref[r : r + 1, cols] = row


def prepare(view, other):
    sessions, feats = view.shape
    return pl.pallas_call(
        prepare_kernel,
        out_shape=(
            jax.ShapeDtypeStruct((sessions, feats), f32),
            jax.ShapeDtypeStruct((sessions, feats), bf16),
            jax.ShapeDtypeStruct((8, feats), f32),
        ),
        compiler_params=params(),
        name="prepare",
    )(view, other)


def finish_kernel(x_size, p0, p1, p2, p3, centered_ref, normed_ref, other_ref, stats_ref, *rest):
    sessions, feats = centered_ref.shape
    out_refs, (high_ref, low_ref, mix_ref, loss_ref) = rest[:4], rest[4:]
    rows = out_refs[0].shape[0]
    my_yl, my_x, my_c = (lax.axis_index(axis) for axis in DP)
    corner, mixed, diag = sum_packed((p0, p1, p2, p3))
    row, col = triangle()
    upper, lower = jnp.where(row < col, mixed, 0.0), jnp.where(row > col, mixed, 0.0)
    top = upper + upper.T + jnp.where(row == col, diag[0:1], 0.0)
    bottom = lower + lower.T + jnp.where(row == col, diag[1:2], 0.0)
    halves = (slice(0, LANES), slice(LANES, 2 * LANES))
    for r, c, part in ((0, 0, top), (0, 1, corner), (1, 0, corner.T), (1, 1, bottom)):
        high = part.astype(bf16)
        high_ref[halves[r], halves[c]] = high
        low_ref[halves[r], halves[c]] = (part - high.astype(f32)).astype(bf16)

    factor = 2.0 * off_weight / sessions
    for k in range(feats // WIDE):
        cols = slice(k * WIDE, (k + 1) * WIDE)
        normed = normed_ref[:, cols]
        mix = jnp.dot(high_ref[...], normed, preferred_element_type=f32)
        mix = mix + jnp.dot(low_ref[...], normed, preferred_element_type=f32)
        mix_ref[...] = mix
        inv, diagonal, mean_other, dot_other = (stats_ref[r : r + 1, cols] for r in range(4))
        shift = 2.0 * (diagonal - 1.0) - 2.0 * off_weight * diagonal
        along = total(mix * centered_ref[:, cols]) / sessions
        mean_all = factor / sessions * total(mix) + shift * mean_other
        dot_all = factor * along + shift * dot_other
        square = along / sessions
        loss = (1.0 - diagonal) * (1.0 - diagonal) + off_weight * (square - diagonal * diagonal)
        for dest, out_ref in enumerate(out_refs):
            chip = (my_yl ^ (dest // 2)) * x_size + my_x
            begin = pl.multiple_of((chip * 2 + (my_c ^ (dest % 2))) * rows, rows)
            mine = pl.ds(begin, rows)
            grad = factor * mix_ref[mine, :] + shift * other_ref[mine, cols].astype(f32)
            out_ref[:, cols] = (inv * (grad - mean_all - centered_ref[mine, cols] * dot_all)).astype(bf16)
        for j in range(WIDE // LANES):
            r = k * (WIDE // LANES) + j
            loss_ref[r : r + 1, :] = loss[:, j * LANES : (j + 1) * LANES]
    high = loss_ref[...].astype(bf16)
    low = (loss_ref[...] - high.astype(f32)).astype(bf16)
    for out_ref in out_refs:
        out_ref[:, feats : feats + LANES] = high
        out_ref[:, feats + LANES :] = low


def finish(parts, centered, normed, other, stats, x_size, rows):
    sessions, feats = centered.shape
    vmem = pl.BlockSpec(memory_space=pltpu.VMEM)
    return pl.pallas_call(
        functools.partial(finish_kernel, x_size),
        in_specs=[vmem] * 8,
        out_specs=[vmem] * 4,
        out_shape=[jax.ShapeDtypeStruct((rows, feats + 2 * LANES), bf16)] * 4,
        scratch_shapes=[
            pltpu.VMEM((sessions, sessions), bf16),
            pltpu.VMEM((sessions, sessions), bf16),
            pltpu.VMEM((sessions, WIDE), f32),
            pltpu.VMEM((feats // LANES, LANES), f32),
        ],
        compiler_params=params(),
        name="finish",
    )(*parts, centered, normed, other, stats)


def unpack_kernel(*refs):
    pieces, (first_ref, second_ref, loss_ref) = refs[:4], refs[4:]
    rows, half = first_ref.shape[0], first_ref.shape[1] // 2
    grads = (first_ref, second_ref)

    def place(my_yl, my_c):
        for source, piece_ref in enumerate(pieces):
            yl, c = my_yl ^ (source // 2), my_c ^ (source % 2)
            grads[c][:, yl * half : (yl + 1) * half] = piece_ref[:, :half].astype(f32)
            if c == 0:
                high, low = piece_ref[:, half : half + LANES], piece_ref[:, half + LANES :]
                loss_ref[yl * rows : (yl + 1) * rows, :] = high.astype(f32) + low.astype(f32)

    here_yl, here_c = lax.axis_index("yl"), lax.axis_index("c")
    for yl in range(2):
        for c in range(2):
            pl.when((here_yl == yl) & (here_c == c))(lambda yl=yl, c=c: place(yl, c))


def unpack(pieces):
    rows, width = pieces[0].shape
    half = width - 2 * LANES
    vmem = pl.BlockSpec(memory_space=pltpu.VMEM)
    grad = jax.ShapeDtypeStruct((rows, 2 * half), f32)
    return pl.pallas_call(
        unpack_kernel,
        in_specs=[vmem] * 4,
        out_shape=(grad, grad, jax.ShapeDtypeStruct((2 * rows, LANES), f32)),
        compiler_params=params(),
        name="unpack",
    )(*pieces)


def on_device(states, token_ids, crop_start, crop_len, item_weight):
    local_rows = states.shape[0]
    x_size = lax.axis_size("x")

    def swap(array):
        return lax.ppermute(array, "c", [(0, 1), (1, 0)])

    keep, send = pool(states, token_ids, crop_start, crop_len, item_weight)
    near, away = collect(*split(keep), swap(send))
    blocks = [near] + [
        lax.ppermute(near if k < x_size else away, CHIPS, [(i, i ^ k) for i in range(2 * x_size)]) for k in CHIP_ORDER
    ]
    packed, other, other_view = gram((0, *CHIP_ORDER), blocks)
    view = swap(other_view)
    packed = add_packed(others(packed, ("yl", "c", "yh"), Y_MOVES))
    centered, normed, stats = prepare(view, other)
    parts = [packed] + [
        lax.ppermute(packed, ("c", "z"), [(c * 4 + z, c * 4 + (z ^ move[c])) for c in range(2) for z in range(4)])
        for move in Z_MOVES
    ]
    pieces = finish(parts, centered, normed, other, stats, x_size, local_rows)
    far = [lax.ppermute(pieces[k], ("yl", "c"), [(i, i ^ k) for i in range(4)]) for k in (2, 3, 1)]
    pieces = [pieces[0], far[2], far[0], far[1]]
    grad_first, grad_second, loss_rows = unpack(pieces)
    return grad_first, grad_second, loss_rows.reshape(-1)


def solution(mesh):
    fine = Mesh(mesh.devices.reshape(2, 4, 2, 2, 4), DP + FEAT)
    placed = (P(DP, None, FEAT), P(DP, None), P(None, DP), P(None, DP), P())
    return jax.shard_map(
        on_device,
        mesh=fine,
        in_specs=placed,
        out_specs=(P(DP, FEAT), P(DP, FEAT), P(FEAT)),
        check_vma=False,
    )
```

```python
import functools

import jax
import jax.numpy as jnp
from jax import lax
from jax.experimental import pallas as pl
from jax.experimental.pallas import tpu as pltpu
from jax.sharding import Mesh
from jax.sharding import PartitionSpec as P

off_weight = 0.0051
eps_norm = 1e-05

f32 = jnp.float32
bf16 = jnp.bfloat16

DP = ("yl", "x", "c")
FEAT = ("yh", "z")
CHIPS = ("yl", "x")
WIDE = 512
POOL_WIDE = 2048
POOL_COPIES = 2
POOL_VMEM = 60
Y_MOVES = ((2, 3), (3, 2), (1, 1))
Z_MOVES = ((1, 3), (3, 1), (2, 2))
LANES = 128


def iota(shape, dim):
    return lax.broadcasted_iota(jnp.int32, shape, dim)


def params(mib=24):
    return pltpu.CompilerParams(vmem_limit_bytes=mib * 1024 * 1024)


def total(values):
    return jnp.sum(values, axis=0, keepdims=True)


def scaled(values):
    count = values.shape[0]
    mean = total(values) / count
    var = total(values * values) / count - mean * mean
    return mean, lax.rsqrt(var + eps_norm)


def coefficient_rows(ids, start, length, table, in_order):
    sessions, tokens = ids.shape
    cols = sessions * tokens
    spread = jnp.where(iota((tokens, cols), 1) % tokens == iota((tokens, cols), 0), 1.0, 0.0).astype(bf16)
    own = iota((sessions, cols), 1) // tokens == iota((sessions, cols), 0)

    def in_line(small):
        rows = jnp.dot(small.astype(f32).astype(bf16), spread, preferred_element_type=f32)
        return total(jnp.where(own, rows, 0.0))

    high, low = in_line(ids // LANES), in_line(ids % LANES)
    place = iota((LANES, cols), 0).astype(f32)
    pick_high = jnp.where(place == high, 1.0, 0.0).astype(bf16)
    first = table.astype(bf16)
    rest = table - first.astype(f32)
    second = rest.astype(bf16)
    third = (rest - second.astype(f32)).astype(bf16)
    found = jnp.zeros((LANES, cols), f32)
    for part in (first, second, third):
        found = found + lax.dot_general(part, pick_high, (((0,), (0,)), ((), ())), preferred_element_type=f32)
    weight = total(jnp.where(place == low, found, 0.0))

    def column(pair):
        first, second = pair[0:1].astype(f32), pair[1:2].astype(f32)
        ordered = (jnp.where(in_order, first, second), jnp.where(in_order, second, first))
        spread_rows = jnp.concatenate([jnp.broadcast_to(row, (sessions, sessions)) for row in ordered], axis=0)
        square = (2 * sessions, sessions)
        mine = iota(square, 0) % sessions == iota(square, 1)
        return jnp.sum(jnp.where(mine, spread_rows, 0.0), axis=1, keepdims=True)

    first_place, past = column(start), column(start + length)
    shape = (2 * sessions, cols)
    col = iota(shape, 1)
    token = (col % tokens).astype(f32)
    inside = (col // tokens == iota(shape, 0) % sessions) & (token >= first_place) & (token < past)
    masked = jnp.where(inside, weight, 0.0)
    return masked / jnp.sum(masked, axis=1, keepdims=True)


def pool_kernel(
    ids_hbm, start_hbm, len_hbm, table_hbm, states_hbm, keep_ref, send_ref,
    ids_ref, start_ref, len_ref, table_ref, states_ref, sums_ref, small_sem, block_sem,
):
    sessions, tokens, feats = states_ref.shape
    pairs = ((ids_hbm, ids_ref), (start_hbm, start_ref), (len_hbm, len_ref), (table_hbm, table_ref))
    small = [pltpu.make_async_copy(src, dst, small_sem.at[i]) for i, (src, dst) in enumerate(pairs)]
    part = sessions // POOL_COPIES
    large = [
        pltpu.make_async_copy(
            states_hbm.at[pl.ds(k * part, part)], states_ref.at[pl.ds(k * part, part)], block_sem.at[k]
        )
        for k in range(POOL_COPIES)
    ]
    for copy in small + large:
        copy.start()
    for copy in small:
        copy.wait()
    coefficients = coefficient_rows(
        ids_ref[...], start_ref[...], len_ref[...], table_ref[...], lax.axis_index("c") == 1
    )
    group = sessions // 2
    for g in range(2):
        own = slice(g * group * tokens, (g + 1) * group * tokens)
        rows = [coefficients[v * sessions + g * group : v * sessions + (g + 1) * group, own] for v in range(2)]
        left = jnp.concatenate(rows, axis=0).astype(bf16)
        for copy in large[g * POOL_COPIES // 2 : (g + 1) * POOL_COPIES // 2]:
            copy.wait()
        for k in range(feats // POOL_WIDE):
            cols = slice(k * POOL_WIDE, (k + 1) * POOL_WIDE)
            block = states_ref[g * group : (g + 1) * group, :, cols].reshape(group * tokens, POOL_WIDE)
            views = jnp.dot(left, block, preferred_element_type=f32)
            if g == 0:
                sums_ref[:, cols] = views
                continue
            early = sums_ref[:, cols]
            for v, out_ref in enumerate((keep_ref, send_ref)):
                rows = slice(v * group, (v + 1) * group)
                out_ref[:, cols] = jnp.concatenate([early[rows], views[rows]], axis=0).astype(bf16)


def pool(states, token_ids, crop_start, crop_len, item_weight):
    sessions, tokens, feats = states.shape
    table = item_weight.reshape(-1, LANES)
    small = (token_ids, crop_start, crop_len, table)
    hbm, vmem = pl.BlockSpec(memory_space=pltpu.HBM), pl.BlockSpec(memory_space=pltpu.VMEM)
    return pl.pallas_call(
        pool_kernel,
        in_specs=[hbm] * 5,
        out_specs=(vmem, vmem),
        out_shape=[jax.ShapeDtypeStruct((sessions, feats), bf16)] * 2,
        scratch_shapes=[pltpu.VMEM(array.shape, array.dtype) for array in (*small, states)]
        + [
            pltpu.VMEM((sessions, feats), f32),
            pltpu.SemaphoreType.DMA((len(small),)),
            pltpu.SemaphoreType.DMA((POOL_COPIES,)),
        ],
        compiler_params=params(POOL_VMEM),
        name="pool",
    )(*small, states)


def split_kernel(mine_ref, near_ref, away_ref):
    half = near_ref.shape[1]
    yl = lax.axis_index("yl")
    for k, out_ref in enumerate((near_ref, away_ref)):
        out_ref[...] = mine_ref[:, pl.ds(pl.multiple_of((yl ^ k) * half, half), half)]


def split(mine):
    rows, feats = mine.shape
    return pl.pallas_call(
        split_kernel,
        out_shape=[jax.ShapeDtypeStruct((rows, feats // 2), bf16)] * 2,
        compiler_params=params(),
        name="split",
    )(mine)


def collect_kernel(mine_near_ref, mine_away_ref, far_ref, near_ref, away_ref):
    rows, half = mine_near_ref.shape
    yl, c = lax.axis_index("yl"), lax.axis_index("c")
    for k, (mine_ref, out_ref) in enumerate(((mine_near_ref, near_ref), (mine_away_ref, away_ref))):
        cols = pl.ds(pl.multiple_of((yl ^ k) * half, half), half)
        out_ref[pl.ds(pl.multiple_of(c * rows, rows), rows), :] = mine_ref[...]
        out_ref[pl.ds(pl.multiple_of((1 - c) * rows, rows), rows), :] = far_ref[:, cols]


def collect(mine_near, mine_away, far):
    rows, half = mine_near.shape
    return pl.pallas_call(
        collect_kernel,
        out_shape=[jax.ShapeDtypeStruct((2 * rows, half), bf16)] * 2,
        compiler_params=params(),
        name="collect",
    )(mine_near, mine_away, far)


def triangle():
    shape = (LANES, LANES)
    return iota(shape, 0), iota(shape, 1)


def store_packed(out_ref, corner, mixed, diag):
    out_ref[0:LANES, :] = corner.astype(bf16)
    out_ref[LANES : 2 * LANES, :] = mixed.astype(bf16)
    first = diag.astype(bf16)
    rest = diag - first.astype(f32)
    second = rest.astype(bf16)
    third = (rest - second.astype(f32)).astype(bf16)
    zeros = jnp.zeros((10, LANES), f32)
    tail = jnp.concatenate([part.astype(f32) for part in (first, second, third)] + [zeros], axis=0)
    out_ref[2 * LANES :, :] = tail.astype(bf16)


def sum_packed(refs):
    body = sum(ref[0 : 2 * LANES, :].astype(f32) for ref in refs)
    tail = sum(ref[2 * LANES :, :].astype(f32) for ref in refs)
    diag = tail[0:2] + tail[2:4] + tail[4:6]
    return body[:LANES], body[LANES:], diag


def gram_kernel(order, *refs):
    block_refs, (packed_ref, normed_ref, view_ref, gram_ref) = refs[: len(order)], refs[len(order) :]
    rows, feats = block_refs[0].shape
    chip = lax.axis_index(CHIPS)
    for k, block_ref in zip(order, block_refs, strict=True):
        view_ref[pl.ds(pl.multiple_of((chip ^ k) * rows, rows), rows), :] = block_ref[...]
    for k in range(feats // WIDE):
        cols = slice(k * WIDE, (k + 1) * WIDE)
        values = view_ref[:, cols].astype(f32)
        mean, inv = scaled(values)
        normed = ((values - mean) * inv).astype(bf16)
        normed_ref[:, cols] = normed
        part = lax.dot_general(normed, normed, (((1,), (1,)), ((), ())), preferred_element_type=f32)
        gram_ref[...] = part if k == 0 else gram_ref[...] + part
    row, col = triangle()
    top, bottom = gram_ref[:LANES, :LANES], gram_ref[LANES:, LANES:]
    diag = jnp.concatenate([total(jnp.where(row == col, part, 0.0)) for part in (top, bottom)], axis=0)
    mixed = jnp.where(row < col, top, jnp.where(row > col, bottom, 0.0))
    store_packed(packed_ref, gram_ref[:LANES, LANES:], mixed, diag)


PACKED = (2 * LANES + 16, LANES)


def gram(order, blocks):
    rows, feats = blocks[0].shape
    sessions = len(blocks) * rows
    whole = jax.ShapeDtypeStruct((sessions, feats), bf16)
    return pl.pallas_call(
        functools.partial(gram_kernel, order),
        out_shape=(jax.ShapeDtypeStruct(PACKED, bf16), whole, whole),
        scratch_shapes=[pltpu.VMEM((sessions, sessions), f32)],
        compiler_params=params(),
        name="gram",
    )(*blocks)


def add_kernel(*refs):
    store_packed(refs[-1], *sum_packed(refs[:-1]))


def add_packed(parts):
    return pl.pallas_call(
        add_kernel,
        out_shape=jax.ShapeDtypeStruct(PACKED, bf16),
        compiler_params=params(),
        name="add_packed",
    )(*parts)


def others(packed, axes, moves):
    parts = [packed]
    for move in moves:
        pairs = []
        for first in range(2):
            for core in range(2):
                for last in range(2):
                    flip = move[core]
                    pairs.append((first * 4 + core * 2 + last, (first ^ (flip // 2)) * 4 + core * 2 + (last ^ (flip % 2))))
        parts.append(lax.ppermute(packed, axes, pairs))
    return parts


def prepare_kernel(view_ref, other_ref, centered_ref, normed_ref, stats_ref):
    sessions, feats = view_ref.shape
    for k in range(feats // WIDE):
        cols = slice(k * WIDE, (k + 1) * WIDE)
        values = view_ref[:, cols].astype(f32)
        other = other_ref[:, cols].astype(f32)
        mean, inv = scaled(values)
        centered = (values - mean) * inv
        normed = centered.astype(bf16)
        centered_ref[:, cols] = centered
        normed_ref[:, cols] = normed
        diagonal = total(normed.astype(f32) * other) / sessions
        rows = [inv, diagonal, total(other) / sessions, total(other * centered) / sessions]
        for r, row in enumerate(rows):
            stats_ref[r : r + 1, cols] = row


def prepare(view, other):
    sessions, feats = view.shape
    return pl.pallas_call(
        prepare_kernel,
        out_shape=(
            jax.ShapeDtypeStruct((sessions, feats), f32),
            jax.ShapeDtypeStruct((sessions, feats), bf16),
            jax.ShapeDtypeStruct((8, feats), f32),
        ),
        compiler_params=params(),
        name="prepare",
    )(view, other)


def finish_kernel(x_size, p0, p1, p2, p3, centered_ref, normed_ref, other_ref, stats_ref, *rest):
    sessions, feats = centered_ref.shape
    out_refs, (high_ref, low_ref, mix_ref, loss_ref) = rest[:4], rest[4:]
    rows = out_refs[0].shape[0]
    my_yl, my_x, my_c = (lax.axis_index(axis) for axis in DP)
    corner, mixed, diag = sum_packed((p0, p1, p2, p3))
    row, col = triangle()
    upper, lower = jnp.where(row < col, mixed, 0.0), jnp.where(row > col, mixed, 0.0)
    top = upper + upper.T + jnp.where(row == col, diag[0:1], 0.0)
    bottom = lower + lower.T + jnp.where(row == col, diag[1:2], 0.0)
    halves = (slice(0, LANES), slice(LANES, 2 * LANES))
    for r, c, part in ((0, 0, top), (0, 1, corner), (1, 0, corner.T), (1, 1, bottom)):
        high = part.astype(bf16)
        high_ref[halves[r], halves[c]] = high
        low_ref[halves[r], halves[c]] = (part - high.astype(f32)).astype(bf16)

    factor = 2.0 * off_weight / sessions
    for k in range(feats // WIDE):
        cols = slice(k * WIDE, (k + 1) * WIDE)
        normed = normed_ref[:, cols]
        mix = jnp.dot(high_ref[...], normed, preferred_element_type=f32)
        mix = mix + jnp.dot(low_ref[...], normed, preferred_element_type=f32)
        mix_ref[...] = mix
        inv, diagonal, mean_other, dot_other = (stats_ref[r : r + 1, cols] for r in range(4))
        shift = 2.0 * (diagonal - 1.0) - 2.0 * off_weight * diagonal
        along = total(mix * centered_ref[:, cols]) / sessions
        mean_all = factor / sessions * total(mix) + shift * mean_other
        dot_all = factor * along + shift * dot_other
        square = along / sessions
        loss = (1.0 - diagonal) * (1.0 - diagonal) + off_weight * (square - diagonal * diagonal)
        for dest, out_ref in enumerate(out_refs):
            chip = (my_yl ^ (dest // 2)) * x_size + my_x
            begin = pl.multiple_of((chip * 2 + (my_c ^ (dest % 2))) * rows, rows)
            mine = pl.ds(begin, rows)
            grad = factor * mix_ref[mine, :] + shift * other_ref[mine, cols].astype(f32)
            out_ref[:, cols] = (inv * (grad - mean_all - centered_ref[mine, cols] * dot_all)).astype(bf16)
        for j in range(WIDE // LANES):
            r = k * (WIDE // LANES) + j
            loss_ref[r : r + 1, :] = loss[:, j * LANES : (j + 1) * LANES]
    high = loss_ref[...].astype(bf16)
    low = (loss_ref[...] - high.astype(f32)).astype(bf16)
    for out_ref in out_refs:
        out_ref[:, feats : feats + LANES] = high
        out_ref[:, feats + LANES :] = low


def finish(parts, centered, normed, other, stats, x_size, rows):
    sessions, feats = centered.shape
    vmem = pl.BlockSpec(memory_space=pltpu.VMEM)
    return pl.pallas_call(
        functools.partial(finish_kernel, x_size),
        in_specs=[vmem] * 8,
        out_specs=[vmem] * 4,
        out_shape=[jax.ShapeDtypeStruct((rows, feats + 2 * LANES), bf16)] * 4,
        scratch_shapes=[
            pltpu.VMEM((sessions, sessions), bf16),
            pltpu.VMEM((sessions, sessions), bf16),
            pltpu.VMEM((sessions, WIDE), f32),
            pltpu.VMEM((feats // LANES, LANES), f32),
        ],
        compiler_params=params(),
        name="finish",
    )(*parts, centered, normed, other, stats)


def unpack_kernel(*refs):
    pieces, (first_ref, second_ref, loss_ref) = refs[:4], refs[4:]
    rows, half = first_ref.shape[0], first_ref.shape[1] // 2
    grads = (first_ref, second_ref)

    def place(my_yl, my_c):
        for source, piece_ref in enumerate(pieces):
            yl, c = my_yl ^ (source // 2), my_c ^ (source % 2)
            grads[c][:, yl * half : (yl + 1) * half] = piece_ref[:, :half].astype(f32)
            if c == 0:
                high, low = piece_ref[:, half : half + LANES], piece_ref[:, half + LANES :]
                loss_ref[yl * rows : (yl + 1) * rows, :] = high.astype(f32) + low.astype(f32)

    here_yl, here_c = lax.axis_index("yl"), lax.axis_index("c")
    for yl in range(2):
        for c in range(2):
            pl.when((here_yl == yl) & (here_c == c))(lambda yl=yl, c=c: place(yl, c))


def unpack(pieces):
    rows, width = pieces[0].shape
    half = width - 2 * LANES
    vmem = pl.BlockSpec(memory_space=pltpu.VMEM)
    grad = jax.ShapeDtypeStruct((rows, 2 * half), f32)
    return pl.pallas_call(
        unpack_kernel,
        in_specs=[vmem] * 4,
        out_shape=(grad, grad, jax.ShapeDtypeStruct((2 * rows, LANES), f32)),
        compiler_params=params(),
        name="unpack",
    )(*pieces)


def on_device(states, token_ids, crop_start, crop_len, item_weight):
    local_rows = states.shape[0]
    x_size = lax.axis_size("x")

    def swap(array):
        return lax.ppermute(array, "c", [(0, 1), (1, 0)])

    keep, send = pool(states, token_ids, crop_start, crop_len, item_weight)
    near, away = collect(*split(keep), swap(send))
    def move(array, k):
        return lax.ppermute(array, CHIPS, [(i, i ^ k) for i in range(2 * x_size)])

    beside = move(away, x_size)
    blocks = [near, beside] + [move(near, k) for k in (2, 3, 1)] + [move(beside, k) for k in (2, 3, 1)]
    packed, other, other_view = gram((0, 4, 2, 3, 1, 6, 7, 5), blocks)
    view = swap(other_view)
    packed = add_packed(others(packed, ("yl", "c", "yh"), Y_MOVES))
    centered, normed, stats = prepare(view, other)
    parts = [packed] + [
        lax.ppermute(packed, ("c", "z"), [(c * 4 + z, c * 4 + (z ^ move[c])) for c in range(2) for z in range(4)])
        for move in Z_MOVES
    ]
    pieces = finish(parts, centered, normed, other, stats, x_size, local_rows)
    far = [lax.ppermute(pieces[k], ("yl", "c"), [(i, i ^ k) for i in range(4)]) for k in (2, 3, 1)]
    pieces = [pieces[0], far[2], far[0], far[1]]
    grad_first, grad_second, loss_rows = unpack(pieces)
    return grad_first, grad_second, loss_rows.reshape(-1)


def solution(mesh):
    fine = Mesh(mesh.devices.reshape(2, 4, 2, 2, 4), DP + FEAT)
    placed = (P(DP, None, FEAT), P(DP, None), P(None, DP), P(None, DP), P())
    return jax.shard_map(
        on_device,
        mesh=fine,
        in_specs=placed,
        out_specs=(P(DP, FEAT), P(DP, FEAT), P(FEAT)),
        check_vma=False,
    )
```

```python
import functools

import jax
import jax.numpy as jnp
from jax import lax
from jax.experimental import pallas as pl
from jax.experimental.pallas import tpu as pltpu
from jax.sharding import Mesh
from jax.sharding import PartitionSpec as P

off_weight = 0.0051
eps_norm = 1e-05

f32 = jnp.float32
bf16 = jnp.bfloat16

DP = ("yl", "x", "c")
FEAT = ("yh", "z")
CHIPS = ("yl", "x")
WIDE = 512
POOL_WIDE = 2048
POOL_COPIES = 2
POOL_VMEM = 60
Y_MOVES = ((2, 3), (3, 2), (1, 1))
Z_MOVES = ((1, 3), (3, 1), (2, 2))
LANES = 128


def iota(shape, dim):
    return lax.broadcasted_iota(jnp.int32, shape, dim)


def params(mib=24):
    return pltpu.CompilerParams(vmem_limit_bytes=mib * 1024 * 1024)


def total(values):
    return jnp.sum(values, axis=0, keepdims=True)


def scaled(values):
    count = values.shape[0]
    mean = total(values) / count
    var = total(values * values) / count - mean * mean
    return mean, lax.rsqrt(var + eps_norm)


def coefficient_rows(ids, start, length, table, in_order):
    sessions, tokens = ids.shape
    cols = sessions * tokens
    spread = jnp.where(iota((tokens, cols), 1) % tokens == iota((tokens, cols), 0), 1.0, 0.0).astype(bf16)
    own = iota((sessions, cols), 1) // tokens == iota((sessions, cols), 0)

    def in_line(small):
        rows = jnp.dot(small.astype(f32).astype(bf16), spread, preferred_element_type=f32)
        return total(jnp.where(own, rows, 0.0))

    high, low = in_line(ids // LANES), in_line(ids % LANES)
    place = iota((LANES, cols), 0).astype(f32)
    pick_high = jnp.where(place == high, 1.0, 0.0).astype(bf16)
    first = table.astype(bf16)
    rest = table - first.astype(f32)
    second = rest.astype(bf16)
    third = (rest - second.astype(f32)).astype(bf16)
    found = jnp.zeros((LANES, cols), f32)
    for part in (first, second, third):
        found = found + lax.dot_general(part, pick_high, (((0,), (0,)), ((), ())), preferred_element_type=f32)
    weight = total(jnp.where(place == low, found, 0.0))

    def column(pair):
        first, second = pair[0:1].astype(f32), pair[1:2].astype(f32)
        ordered = (jnp.where(in_order, first, second), jnp.where(in_order, second, first))
        spread_rows = jnp.concatenate([jnp.broadcast_to(row, (sessions, sessions)) for row in ordered], axis=0)
        square = (2 * sessions, sessions)
        mine = iota(square, 0) % sessions == iota(square, 1)
        return jnp.sum(jnp.where(mine, spread_rows, 0.0), axis=1, keepdims=True)

    first_place, past = column(start), column(start + length)
    shape = (2 * sessions, cols)
    col = iota(shape, 1)
    token = (col % tokens).astype(f32)
    inside = (col // tokens == iota(shape, 0) % sessions) & (token >= first_place) & (token < past)
    masked = jnp.where(inside, weight, 0.0)
    return masked / jnp.sum(masked, axis=1, keepdims=True)


def pool_kernel(
    ids_hbm, start_hbm, len_hbm, table_hbm, states_hbm, keep_ref, send_ref,
    ids_ref, start_ref, len_ref, table_ref, states_ref, sums_ref, small_sem, block_sem,
):
    sessions, tokens, feats = states_ref.shape
    pairs = ((ids_hbm, ids_ref), (start_hbm, start_ref), (len_hbm, len_ref), (table_hbm, table_ref))
    small = [pltpu.make_async_copy(src, dst, small_sem.at[i]) for i, (src, dst) in enumerate(pairs)]
    part = sessions // POOL_COPIES
    large = [
        pltpu.make_async_copy(
            states_hbm.at[pl.ds(k * part, part)], states_ref.at[pl.ds(k * part, part)], block_sem.at[k]
        )
        for k in range(POOL_COPIES)
    ]
    for copy in small + large:
        copy.start()
    for copy in small:
        copy.wait()
    coefficients = coefficient_rows(
        ids_ref[...], start_ref[...], len_ref[...], table_ref[...], lax.axis_index("c") == 1
    )
    group = sessions // 2
    for g in range(2):
        own = slice(g * group * tokens, (g + 1) * group * tokens)
        rows = [coefficients[v * sessions + g * group : v * sessions + (g + 1) * group, own] for v in range(2)]
        left = jnp.concatenate(rows, axis=0).astype(bf16)
        for copy in large[g * POOL_COPIES // 2 : (g + 1) * POOL_COPIES // 2]:
            copy.wait()
        for k in range(feats // POOL_WIDE):
            cols = slice(k * POOL_WIDE, (k + 1) * POOL_WIDE)
            block = states_ref[g * group : (g + 1) * group, :, cols].reshape(group * tokens, POOL_WIDE)
            views = jnp.dot(left, block, preferred_element_type=f32)
            if g == 0:
                sums_ref[:, cols] = views
                continue
            early = sums_ref[:, cols]
            for v, out_ref in enumerate((keep_ref, send_ref)):
                rows = slice(v * group, (v + 1) * group)
                out_ref[:, cols] = jnp.concatenate([early[rows], views[rows]], axis=0).astype(bf16)


def pool(states, token_ids, crop_start, crop_len, item_weight):
    sessions, tokens, feats = states.shape
    table = item_weight.reshape(-1, LANES)
    small = (token_ids, crop_start, crop_len, table)
    hbm, vmem = pl.BlockSpec(memory_space=pltpu.HBM), pl.BlockSpec(memory_space=pltpu.VMEM)
    return pl.pallas_call(
        pool_kernel,
        in_specs=[hbm] * 5,
        out_specs=(vmem, vmem),
        out_shape=[jax.ShapeDtypeStruct((sessions, feats), bf16)] * 2,
        scratch_shapes=[pltpu.VMEM(array.shape, array.dtype) for array in (*small, states)]
        + [
            pltpu.VMEM((sessions, feats), f32),
            pltpu.SemaphoreType.DMA((len(small),)),
            pltpu.SemaphoreType.DMA((POOL_COPIES,)),
        ],
        compiler_params=params(POOL_VMEM),
        name="pool",
    )(*small, states)


def split_kernel(mine_ref, near_ref, away_ref):
    half = near_ref.shape[1]
    yl = lax.axis_index("yl")
    for k, out_ref in enumerate((near_ref, away_ref)):
        out_ref[...] = mine_ref[:, pl.ds(pl.multiple_of((yl ^ k) * half, half), half)]


def split(mine):
    rows, feats = mine.shape
    return pl.pallas_call(
        split_kernel,
        out_shape=[jax.ShapeDtypeStruct((rows, feats // 2), bf16)] * 2,
        compiler_params=params(),
        name="split",
    )(mine)


def collect_kernel(mine_near_ref, mine_away_ref, far_ref, near_ref, away_ref):
    rows, half = mine_near_ref.shape
    yl, c = lax.axis_index("yl"), lax.axis_index("c")
    for k, (mine_ref, out_ref) in enumerate(((mine_near_ref, near_ref), (mine_away_ref, away_ref))):
        cols = pl.ds(pl.multiple_of((yl ^ k) * half, half), half)
        out_ref[pl.ds(pl.multiple_of(c * rows, rows), rows), :] = mine_ref[...]
        out_ref[pl.ds(pl.multiple_of((1 - c) * rows, rows), rows), :] = far_ref[:, cols]


def collect(mine_near, mine_away, far):
    rows, half = mine_near.shape
    return pl.pallas_call(
        collect_kernel,
        out_shape=[jax.ShapeDtypeStruct((2 * rows, half), bf16)] * 2,
        compiler_params=params(),
        name="collect",
    )(mine_near, mine_away, far)


def triangle():
    shape = (LANES, LANES)
    return iota(shape, 0), iota(shape, 1)


def store_packed(out_ref, corner, mixed, diag):
    out_ref[0:LANES, :] = corner.astype(bf16)
    out_ref[LANES : 2 * LANES, :] = mixed.astype(bf16)
    first = diag.astype(bf16)
    rest = diag - first.astype(f32)
    second = rest.astype(bf16)
    third = (rest - second.astype(f32)).astype(bf16)
    zeros = jnp.zeros((10, LANES), f32)
    tail = jnp.concatenate([part.astype(f32) for part in (first, second, third)] + [zeros], axis=0)
    out_ref[2 * LANES :, :] = tail.astype(bf16)


def sum_packed(refs):
    body = sum(ref[0 : 2 * LANES, :].astype(f32) for ref in refs)
    tail = sum(ref[2 * LANES :, :].astype(f32) for ref in refs)
    diag = tail[0:2] + tail[2:4] + tail[4:6]
    return body[:LANES], body[LANES:], diag


def gram_kernel(order, *refs):
    block_refs, (packed_ref, normed_ref, view_ref, gram_ref) = refs[: len(order)], refs[len(order) :]
    rows, feats = block_refs[0].shape
    chip = lax.axis_index(CHIPS)
    for k, block_ref in zip(order, block_refs, strict=True):
        view_ref[pl.ds(pl.multiple_of((chip ^ k) * rows, rows), rows), :] = block_ref[...]
    for k in range(feats // WIDE):
        cols = slice(k * WIDE, (k + 1) * WIDE)
        values = view_ref[:, cols].astype(f32)
        mean, inv = scaled(values)
        normed = ((values - mean) * inv).astype(bf16)
        normed_ref[:, cols] = normed
        part = lax.dot_general(normed, normed, (((1,), (1,)), ((), ())), preferred_element_type=f32)
        gram_ref[...] = part if k == 0 else gram_ref[...] + part
    row, col = triangle()
    top, bottom = gram_ref[:LANES, :LANES], gram_ref[LANES:, LANES:]
    diag = jnp.concatenate([total(jnp.where(row == col, part, 0.0)) for part in (top, bottom)], axis=0)
    mixed = jnp.where(row < col, top, jnp.where(row > col, bottom, 0.0))
    store_packed(packed_ref, gram_ref[:LANES, LANES:], mixed, diag)


PACKED = (2 * LANES + 16, LANES)


def gram(order, blocks):
    rows, feats = blocks[0].shape
    sessions = len(blocks) * rows
    whole = jax.ShapeDtypeStruct((sessions, feats), bf16)
    return pl.pallas_call(
        functools.partial(gram_kernel, order),
        out_shape=(jax.ShapeDtypeStruct(PACKED, bf16), whole, whole),
        scratch_shapes=[pltpu.VMEM((sessions, sessions), f32)],
        compiler_params=params(),
        name="gram",
    )(*blocks)


def add_kernel(*refs):
    store_packed(refs[-1], *sum_packed(refs[:-1]))


def add_packed(parts):
    return pl.pallas_call(
        add_kernel,
        out_shape=jax.ShapeDtypeStruct(PACKED, bf16),
        compiler_params=params(),
        name="add_packed",
    )(*parts)


def others(packed, axes, moves):
    parts = [packed]
    for move in moves:
        pairs = []
        for first in range(2):
            for core in range(2):
                for last in range(2):
                    flip = move[core]
                    pairs.append((first * 4 + core * 2 + last, (first ^ (flip // 2)) * 4 + core * 2 + (last ^ (flip % 2))))
        parts.append(lax.ppermute(packed, axes, pairs))
    return parts


def prepare_kernel(view_ref, other_ref, centered_ref, normed_ref, stats_ref):
    sessions, feats = view_ref.shape
    for k in range(feats // WIDE):
        cols = slice(k * WIDE, (k + 1) * WIDE)
        values = view_ref[:, cols].astype(f32)
        other = other_ref[:, cols].astype(f32)
        mean, inv = scaled(values)
        centered = (values - mean) * inv
        normed = centered.astype(bf16)
        centered_ref[:, cols] = centered
        normed_ref[:, cols] = normed
        diagonal = total(normed.astype(f32) * other) / sessions
        rows = [inv, diagonal, total(other) / sessions, total(other * centered) / sessions]
        for r, row in enumerate(rows):
            stats_ref[r : r + 1, cols] = row


def prepare(view, other):
    sessions, feats = view.shape
    return pl.pallas_call(
        prepare_kernel,
        out_shape=(
            jax.ShapeDtypeStruct((sessions, feats), f32),
            jax.ShapeDtypeStruct((sessions, feats), bf16),
            jax.ShapeDtypeStruct((8, feats), f32),
        ),
        compiler_params=params(),
        name="prepare",
    )(view, other)


def finish_kernel(x_size, p0, p1, p2, p3, centered_ref, normed_ref, other_ref, stats_ref, *rest):
    sessions, feats = centered_ref.shape
    out_refs, (high_ref, low_ref, mix_ref, loss_ref) = rest[:4], rest[4:]
    rows = out_refs[0].shape[0]
    my_yl, my_x, my_c = (lax.axis_index(axis) for axis in DP)
    corner, mixed, diag = sum_packed((p0, p1, p2, p3))
    row, col = triangle()
    upper, lower = jnp.where(row < col, mixed, 0.0), jnp.where(row > col, mixed, 0.0)
    top = upper + upper.T + jnp.where(row == col, diag[0:1], 0.0)
    bottom = lower + lower.T + jnp.where(row == col, diag[1:2], 0.0)
    halves = (slice(0, LANES), slice(LANES, 2 * LANES))
    for r, c, part in ((0, 0, top), (0, 1, corner), (1, 0, corner.T), (1, 1, bottom)):
        high = part.astype(bf16)
        high_ref[halves[r], halves[c]] = high
        low_ref[halves[r], halves[c]] = (part - high.astype(f32)).astype(bf16)

    factor = 2.0 * off_weight / sessions
    for k in range(feats // WIDE):
        cols = slice(k * WIDE, (k + 1) * WIDE)
        normed = normed_ref[:, cols]
        mix = jnp.dot(high_ref[...], normed, preferred_element_type=f32)
        mix = mix + jnp.dot(low_ref[...], normed, preferred_element_type=f32)
        mix_ref[...] = mix
        inv, diagonal, mean_other, dot_other = (stats_ref[r : r + 1, cols] for r in range(4))
        shift = 2.0 * (diagonal - 1.0) - 2.0 * off_weight * diagonal
        along = total(mix * centered_ref[:, cols]) / sessions
        mean_all = factor / sessions * total(mix) + shift * mean_other
        dot_all = factor * along + shift * dot_other
        square = along / sessions
        loss = (1.0 - diagonal) * (1.0 - diagonal) + off_weight * (square - diagonal * diagonal)
        for dest, out_ref in enumerate(out_refs):
            chip = (my_yl ^ (dest // 2)) * x_size + my_x
            begin = pl.multiple_of((chip * 2 + (my_c ^ (dest % 2))) * rows, rows)
            mine = pl.ds(begin, rows)
            grad = factor * mix_ref[mine, :] + shift * other_ref[mine, cols].astype(f32)
            out_ref[:, cols] = (inv * (grad - mean_all - centered_ref[mine, cols] * dot_all)).astype(bf16)
        for j in range(WIDE // LANES):
            r = k * (WIDE // LANES) + j
            loss_ref[r : r + 1, :] = loss[:, j * LANES : (j + 1) * LANES]
    high = loss_ref[...].astype(bf16)
    low = (loss_ref[...] - high.astype(f32)).astype(bf16)
    for out_ref in out_refs:
        out_ref[:, feats : feats + LANES] = high
        out_ref[:, feats + LANES :] = low


def finish(parts, centered, normed, other, stats, x_size, rows):
    sessions, feats = centered.shape
    vmem = pl.BlockSpec(memory_space=pltpu.VMEM)
    return pl.pallas_call(
        functools.partial(finish_kernel, x_size),
        in_specs=[vmem] * 8,
        out_specs=[vmem] * 4,
        out_shape=[jax.ShapeDtypeStruct((rows, feats + 2 * LANES), bf16)] * 4,
        scratch_shapes=[
            pltpu.VMEM((sessions, sessions), bf16),
            pltpu.VMEM((sessions, sessions), bf16),
            pltpu.VMEM((sessions, WIDE), f32),
            pltpu.VMEM((feats // LANES, LANES), f32),
        ],
        compiler_params=params(),
        name="finish",
    )(*parts, centered, normed, other, stats)


def unpack_kernel(p0, p1, p2, p3, first_hbm, second_hbm, loss_hbm, grads_ref, loss_ref, sem):
    pieces = (p0, p1, p2, p3)
    rows, half = p0.shape[0], first_hbm.shape[1] // 2
    here_yl, here_c = lax.axis_index("yl"), lax.axis_index("c")

    def place(my_yl, my_c):
        copies = []
        for source, piece_ref in enumerate(pieces):
            yl, c = my_yl ^ (source // 2), my_c ^ (source % 2)
            cols = slice(yl * half, (yl + 1) * half)
            if c == 0:
                high, low = piece_ref[:, half : half + LANES], piece_ref[:, half + LANES :]
                loss_ref[yl * rows : (yl + 1) * rows, :] = high.astype(f32) + low.astype(f32)
            grads_ref[c, :, cols] = piece_ref[:, :half].astype(f32)
            to = (first_hbm, second_hbm)[c]
            copies.append(pltpu.make_async_copy(grads_ref.at[c, :, cols], to.at[:, cols], sem.at[source]))
            copies[-1].start()
        copies.append(pltpu.make_async_copy(loss_ref, loss_hbm, sem.at[4]))
        copies[-1].start()
        for copy in copies:
            copy.wait()

    for yl in range(2):
        for c in range(2):
            pl.when((here_yl == yl) & (here_c == c))(lambda yl=yl, c=c: place(yl, c))


def unpack(pieces):
    rows, width = pieces[0].shape
    half = width - 2 * LANES
    vmem, hbm = pl.BlockSpec(memory_space=pltpu.VMEM), pl.BlockSpec(memory_space=pltpu.HBM)
    grad = jax.ShapeDtypeStruct((rows, 2 * half), f32)
    return pl.pallas_call(
        unpack_kernel,
        in_specs=[vmem] * 4,
        out_specs=(hbm, hbm, hbm),
        out_shape=(grad, grad, jax.ShapeDtypeStruct((2 * rows, LANES), f32)),
        scratch_shapes=[
            pltpu.VMEM((2, rows, 2 * half), f32),
            pltpu.VMEM((2 * rows, LANES), f32),
            pltpu.SemaphoreType.DMA((5,)),
        ],
        compiler_params=params(),
        name="unpack",
    )(*pieces)


def on_device(states, token_ids, crop_start, crop_len, item_weight):
    local_rows = states.shape[0]
    x_size = lax.axis_size("x")

    def swap(array):
        return lax.ppermute(array, "c", [(0, 1), (1, 0)])

    keep, send = pool(states, token_ids, crop_start, crop_len, item_weight)
    near, away = collect(*split(keep), swap(send))
    def move(array, k):
        return lax.ppermute(array, CHIPS, [(i, i ^ k) for i in range(2 * x_size)])

    beside = move(away, x_size)
    blocks = [near, beside] + [move(near, k) for k in (2, 3, 1)] + [move(beside, k) for k in (2, 3, 1)]
    packed, other, other_view = gram((0, 4, 2, 3, 1, 6, 7, 5), blocks)
    view = swap(other_view)
    packed = add_packed(others(packed, ("yl", "c", "yh"), Y_MOVES))
    centered, normed, stats = prepare(view, other)
    parts = [packed] + [
        lax.ppermute(packed, ("c", "z"), [(c * 4 + z, c * 4 + (z ^ move[c])) for c in range(2) for z in range(4)])
        for move in Z_MOVES
    ]
    pieces = finish(parts, centered, normed, other, stats, x_size, local_rows)
    far = [lax.ppermute(pieces[k], ("yl", "c"), [(i, i ^ k) for i in range(4)]) for k in (2, 3, 1)]
    pieces = [pieces[0], far[2], far[0], far[1]]
    grad_first, grad_second, loss_rows = unpack(pieces)
    return grad_first, grad_second, loss_rows.reshape(-1)


def solution(mesh):
    fine = Mesh(mesh.devices.reshape(2, 4, 2, 2, 4), DP + FEAT)
    placed = (P(DP, None, FEAT), P(DP, None), P(None, DP), P(None, DP), P())
    return jax.shard_map(
        on_device,
        mesh=fine,
        in_specs=placed,
        out_specs=(P(DP, FEAT), P(DP, FEAT), P(FEAT)),
        check_vma=False,
    )
```
